256 devices in a mesh: diag: 32 (over z_lo, x, y), off: 8 (over z_hi, core).
Axes of the slice: x: 4, y: 4, z: 8 (z_hi: 4, z_lo: 2; z = z_hi * 2 + z_lo), core: 2. Of those that a mesh axis runs over, the one named last changes fastest.
Arguments:
- features: bfloat16 [4096, 256], P('diag'), may hold values from -6 to 6
- conv_weight: bfloat16 [2, 3, 256, 128], replicated, may hold values from -0.21875 to 0.21875
- out_weight: bfloat16 [2, 128, 256], replicated, may hold values from -0.5 to 0.5
- proj_weight: bfloat16 [256, 128], replicated, may hold values from -0.375 to 0.375
- offset_embed: bfloat16 [512, 64], P('off'), may hold values from -6 to 6
- pair_filter_weight: bfloat16 [2, 3, 3, 64, 64], replicated, may hold values from -0.25 to 0.25
- head_weight: float32 [64], replicated, may hold values from -0.75 to 0.75
- target: float32 [512, 4096], P('off', 'diag'), may hold values from -6 to 6
- cell_mask: int32 [512, 4096], P('off', 'diag'), may hold values 0 or 1
Outputs:
- prediction: float32 [512, 4096], P('off', 'diag')
- loss: float32 [], replicated
The draws below stay inside these ranges and needn't reach their ends.
All inputs are finite; a program needn't handle non-finite values. No bound on the sum of `cell_mask` on one device may be relied on, other than what follows from the above.
Results may differ from the reference program's by a relative error of at most 0.008.
Values may be sent and summed in bfloat16 or wider, within the bound.
A program may use at most 128 MiB of HBM per device.

```python
import jax
import jax.numpy as jnp
from jax import lax

D = 256
INNER = 128
CP = 64
BAND = 512
BINS_PER_DEVICE = 128
FIRST_DILATION = 4
SECOND_DILATION = 8
PAIR_DILATION = 4
BINS = 4096
N_DIAG = 32


def with_ends(array, key, smallest, largest):
    longest = array.shape.index(max(array.shape))
    spots = []
    for shift in (0, 1):
        where = [jax.random.randint(jax.random.fold_in(key, axis), (), 0, length) for axis, length in enumerate(array.shape)]
        where[longest] = (where[longest] + shift) % array.shape[longest]
        spots.append(tuple(where))
    return array.at[spots[0]].set(smallest).at[spots[1]].set(largest)


def levels(key, dims, split, smallest, largest):
    def one(position, parts):
        draws = jax.random.uniform(jax.random.fold_in(jax.random.fold_in(key, 6), position), (parts,), jnp.float32, smallest / len(split), largest / len(split))
        return jnp.repeat(jnp.exp(draws), dims[position] // parts).reshape((-1,) + (1,) * (len(dims) - position - 1))

    level = one(*split[0])
    for cut in split[1:]:
        level = level * one(*cut)
    return level


def bell_draw(stream_key, dims, width, reach, split=(), kind=jnp.bfloat16):
    factor_of = levels(stream_key, dims, split, -0.22, 0.18) if split else 1.0
    entries = jax.random.normal(stream_key, dims, jnp.float32) * width * factor_of
    return jnp.minimum(jnp.maximum(entries, -reach), reach).astype(kind)


def setup_inputs(seed: int = 0) -> dict:
    keys = jax.random.split(jax.random.key(seed), 10)
    features = bell_draw(keys[0], (BINS, D), 1.0, 6.0, ((0, 32),))
    conv_weight = bell_draw(keys[1], (2, 3, D, INNER), (3 * D) ** -0.5, 0.21875)
    out_weight = bell_draw(keys[2], (2, INNER, D), INNER ** -0.5, 0.5)
    proj_weight = bell_draw(keys[3], (D, 2 * CP), D ** -0.5, 0.375)
    offset_embed = bell_draw(keys[4], (BAND, CP), 1.0, 6.0, ((0, 8),))
    pair_filter_weight = bell_draw(keys[5], (2, 3, 3, CP, CP), (9 * CP) ** -0.5, 0.25)
    head_weight = bell_draw(keys[6], (CP,), CP ** -0.5, 0.75, (), jnp.float32)
    target = bell_draw(keys[7], (BAND, BINS), 1.0, 6.0, ((0, 8), (1, 32)), jnp.float32)
    cell_mask = with_ends((jax.random.randint(keys[8], (BAND, BINS), 0, 4) < 3).astype(jnp.int32), jax.random.fold_in(keys[8], 1), 0, 1)
    return {"features": features, "conv_weight": conv_weight, "out_weight": out_weight, "proj_weight": proj_weight, "offset_embed": offset_embed, "pair_filter_weight": pair_filter_weight, "head_weight": head_weight, "target": target, "cell_mask": cell_mask}


def filter_taps(field, weight, spread_rows):
    chans, rows_off, rows_bin = field.shape
    out_off = rows_off - 2 * spread_rows
    out_bin = rows_bin - 2 * spread_rows
    accum = jnp.zeros((weight.shape[2], out_off * out_bin), jnp.float32)
    for tap_off in range(3):
        for tap_bin in range(3):
            piece = field[:, tap_off * spread_rows:tap_off * spread_rows + out_off, tap_bin * spread_rows:tap_bin * spread_rows + out_bin]
            piece = piece.reshape(chans, out_off * out_bin)
            accum = accum + jnp.dot(weight[tap_off, tap_bin], piece, preferred_element_type=jnp.float32)
    return accum.reshape(weight.shape[2], out_off, out_bin)


def trunk_layer(rows, padded, conv, outw, spread_rows):
    count = rows.shape[0]
    accum = jnp.zeros((count, conv.shape[2]), jnp.float32)
    for tap in range(3):
        accum = accum + jnp.dot(padded[tap * spread_rows:tap * spread_rows + count], conv[tap], preferred_element_type=jnp.float32)
    interior = jax.nn.relu(accum).astype(jnp.bfloat16)
    return (rows.astype(jnp.float32) + jnp.dot(interior, outw, preferred_element_type=jnp.float32)).astype(jnp.bfloat16)


def reference(features, conv_weight, out_weight, proj_weight, offset_embed, pair_filter_weight, head_weight, target, cell_mask):
    total_bins = BINS_PER_DEVICE * N_DIAG
    hidden = features
    for layer_apply, spread_rows in enumerate((FIRST_DILATION, SECOND_DILATION)):
        padded = jnp.pad(jax.nn.relu(hidden), ((spread_rows, spread_rows), (0, 0)))
        hidden = trunk_layer(hidden, padded, conv_weight[layer_apply], out_weight[layer_apply], spread_rows)
    projected = jnp.dot(hidden, proj_weight, preferred_element_type=jnp.float32).astype(jnp.bfloat16)
    left = projected[:, :CP]
    right = projected[:, CP:]
    widen_rows = 2 * PAIR_DILATION
    span_width = BINS_PER_DEVICE + 2 * widen_rows
    left_pad = jnp.pad(left, ((widen_rows, widen_rows), (0, 0)))
    right_pad = jnp.pad(right, ((widen_rows, widen_rows + BAND), (0, 0)))
    index_grid = jnp.arange(BAND, dtype=jnp.int32)[:, None] + jnp.arange(span_width, dtype=jnp.int32)[None, :]
    embed_t = offset_embed.T.astype(jnp.float32)

    def one_block(block):
        start_index = (block * BINS_PER_DEVICE).astype(jnp.int32)
        left_ext = lax.dynamic_slice_in_dim(left_pad, start_index, span_width, 0)
        right_ext = lax.dynamic_slice_in_dim(right_pad, start_index, span_width + BAND - 1, 0)
        gathered = jnp.take(right_ext.T, index_grid, axis=1)
        total = gathered.astype(jnp.float32) + left_ext.T.astype(jnp.float32)[:, None, :] + embed_t[:, :, None]
        where_bin = start_index - widen_rows + jnp.arange(span_width, dtype=jnp.int32)
        inside = ((where_bin >= 0) & (where_bin < total_bins)).astype(jnp.float32)
        pair_block = (jax.nn.relu(total) * inside[None, None, :]).astype(jnp.bfloat16)
        first_layer = filter_taps(jnp.pad(pair_block, ((0, 0), (PAIR_DILATION, PAIR_DILATION), (0, 0))), pair_filter_weight[0], PAIR_DILATION)
        interior_bin = start_index - PAIR_DILATION + jnp.arange(BINS_PER_DEVICE + 2 * PAIR_DILATION, dtype=jnp.int32)
        inside_inner = ((interior_bin >= 0) & (interior_bin < total_bins)).astype(jnp.float32)
        interior = (jax.nn.relu(first_layer) * inside_inner[None, None, :]).astype(jnp.bfloat16)
        second_layer = filter_taps(jnp.pad(interior, ((0, 0), (PAIR_DILATION, PAIR_DILATION), (0, 0))), pair_filter_weight[1], PAIR_DILATION)
        result = pair_block[:, :, widen_rows:widen_rows + BINS_PER_DEVICE].astype(jnp.float32) + second_layer
        return jnp.sum(result * head_weight[:, None, None], 0)

    blocks = lax.map(one_block, jnp.arange(N_DIAG, dtype=jnp.int32))
    prediction = jnp.transpose(blocks, (1, 0, 2)).reshape(BAND, total_bins)
    within = (jnp.arange(BAND, dtype=jnp.int32)[:, None] + jnp.arange(total_bins, dtype=jnp.int32)[None, :]) < total_bins
    valid = cell_mask.astype(jnp.float32) * within.astype(jnp.float32)
    loss = jnp.sum(valid * (prediction - target) ** 2) / (BAND * total_bins)
    return prediction, loss
```

```python
import functools

import jax
import jax.numpy as jnp
import ml_dtypes
import numpy as np
from jax import lax
from jax.experimental import pallas as pl
from jax.experimental.pallas import tpu as pltpu
from jax.sharding import PartitionSpec as P

BINS = 4096
BAND = 512
CP = 64
D = 256
N_DIAG = 32
N_OFF = 8
W_LEFT = 192
W_RIGHT = 256
ROWS = W_LEFT + W_RIGHT
F32 = jnp.float32
BF16 = jnp.bfloat16
NT = (((1,), (1,)), ((), ()))


def selections():
    def one_hot(index, width):
        index = np.asarray(index).reshape(-1)
        return (index[:, None] == np.arange(width)[None, :]).astype(ml_dtypes.bfloat16)

    par, v, r, s = np.meshgrid(np.arange(2), np.arange(27), np.arange(4), np.arange(4), indexing="ij")
    right = one_hot(4 * (2 * v + par) + r + s + 16, W_RIGHT)
    par, jj, r, s = np.meshgrid(np.arange(2), np.arange(18), np.arange(4), np.arange(4), indexing="ij")
    left = one_hot(4 * (2 * jj + par) + s + 24, W_LEFT)
    m, r, s = np.meshgrid(np.arange(10), np.arange(4), np.arange(4), indexing="ij")
    embed = one_hot(8 * m + r + 8, 96)
    jo, jj, r, s = np.meshgrid(np.arange(2), np.arange(16), np.arange(4), np.arange(4), indexing="ij")
    back = one_hot(r * 128 + 4 * (2 * jj + jo) + s, 512)
    return right, left, embed, back


def dot(a, b):
    return jnp.dot(a, b, preferred_element_type=F32)


def dot_nt(a, b):
    return lax.dot_general(a, b, NT, preferred_element_type=F32)


def kernel(
    feat, conv, outw, proj, emb, filt, head, target, mask, sel_r, sel_l, sel_e, sel_b,
    pred, loss,
    win, ewin, wconv, wout, wproj, wfilt, vtarget, vmask, vsel_r, vsel_l, vsel_e, vsel_b,
    first, gin, gpair, rr, ll, ee, pair, inner, red1, red2,
    local_sem, send_sem, recv_sem, self_sem, s1, r1, s2, r2,
):
    d = lax.axis_index("diag")
    g = lax.axis_index("off")
    h = g // 2
    odd = g % 2

    left_moves = [(0, -1, 96, 32, 0), (1, 1, 0, 32, 160)]
    even_moves = [(2, h - 1, 96, 32, 192), (3, h, 0, 128, 224), (4, h + 1, 0, 96, 352)]
    odd_moves = [(2, h, 32, 96, 192), (3, h + 1, 0, 128, 288), (4, h + 2, 0, 32, 416)]
    embed_moves = [(5, -1, 48, 0), (6, 1, 0, 80)]

    def sends_to(ahead):
        return jnp.logical_and(d - ahead >= 0, d - ahead < N_DIAG)

    def hears_from(ahead):
        return jnp.logical_and(d + ahead >= 0, d + ahead < N_DIAG)

    def move(number, ahead, start, count, to):
        return pltpu.make_async_remote_copy(
            src_ref=feat.at[pl.ds(start, count)],
            dst_ref=win.at[pl.ds(to, count)],
            send_sem=send_sem.at[number],
            recv_sem=recv_sem.at[number],
            device_id=(d - ahead, g),
            device_id_type=pl.DeviceIdType.MESH,
        )

    def own_move(start, count, to):
        return pltpu.make_async_copy(feat.at[pl.ds(start, count)], win.at[pl.ds(to, count)], self_sem)

    def embed_move(number, ahead, start, to):
        return pltpu.make_async_remote_copy(
            src_ref=emb.at[pl.ds(start, 16)],
            dst_ref=ewin.at[pl.ds(to, 16)],
            send_sem=send_sem.at[number],
            recv_sem=recv_sem.at[number],
            device_id=(d, g - ahead),
            device_id_type=pl.DeviceIdType.MESH,
        )

    barrier = pltpu.get_barrier_semaphore()

    def greet(peer_d, peer_g):
        pl.semaphore_signal(barrier, inc=1, device_id=(peer_d, peer_g), device_id_type=pl.DeviceIdType.MESH)

    def away(ahead):
        return ahead != 0 if not isinstance(ahead, int) else True

    def count_of(cond):
        return jnp.where(cond, 1, 0).astype(jnp.int32)

    total = jnp.int32(30)
    for reach in (-1, 1):
        ok_s = jnp.logical_and(d - reach >= 0, d - reach < N_DIAG)

        @pl.when(ok_s)
        def _(reach=reach):
            greet(d - reach, g)
            greet(d - reach, g)

        total = total + 2 * count_of(ok_s)
        ok_g = jnp.logical_and(g - reach >= 0, g - reach < N_OFF)

        @pl.when(ok_g)
        def _(reach=reach):
            greet(d, g - reach)
            greet(d, g - reach)

        total = total + 2 * count_of(ok_g)
    for step in range(3):
        ahead = h - 1 + odd + step
        ok_s = jnp.logical_and(sends_to(ahead), ahead != 0)
        ok_r = jnp.logical_and(hears_from(ahead), ahead != 0)

        @pl.when(ok_s)
        def _(ahead=ahead):
            greet(d - ahead, g)

        @pl.when(ok_r)
        def _(ahead=ahead):
            greet(d + ahead, g)

        total = total + count_of(ok_s) + count_of(ok_r)

    t1 = (d // 16) * 8 + g
    t2 = d % 16

    def peer1(k):
        t = (t1 + k) % 16
        return t, ((t // 8) * 16 + t2, t % 8)

    def peer2(k):
        t = (t2 + k) % 16
        return t, ((d // 16) * 16 + t, g)

    def greet_both(k, carry):
        greet(*peer1(k)[1])
        greet(*peer2(k)[1])
        return carry

    lax.fori_loop(1, 16, greet_both, 0)

    loads = [(feat, win.at[pl.ds(32, 128)])]
    loads += [(emb, ewin.at[pl.ds(16, 64)])]
    loads += [(filt, wfilt)]
    for layer in range(2):
        for tap in range(3):
            loads.append((conv.at[layer, tap], wconv.at[layer, :, pl.ds(128 * tap, 128)]))
    loads += [(outw, wout), (proj, wproj), (sel_r, vsel_r), (sel_l, vsel_l), (sel_e, vsel_e), (sel_b, vsel_b)]
    loads += [(target, vtarget), (mask, vmask)]
    copies = [pltpu.make_async_copy(a, b, local_sem.at[i]) for i, (a, b) in enumerate(loads)]
    for copy in copies:
        copy.start()

    pl.semaphore_wait(barrier, total)

    def run_moves(moves, act):
        for number, ahead, start, count, to in moves:
            act(number, ahead, start, count, to)

    def begin(number, ahead, start, count, to):
        if isinstance(ahead, int):
            pl.when(sends_to(ahead))(lambda: move(number, ahead, start, count, to).start())
            return
        pl.when(jnp.logical_and(sends_to(ahead), ahead != 0))(
            lambda: move(number, ahead, start, count, to).start()
        )
        pl.when(ahead == 0)(lambda: own_move(start, count, to).start())

    def finish(number, ahead, start, count, to):
        if isinstance(ahead, int):
            pl.when(hears_from(ahead))(lambda: move(number, ahead, start, count, to).wait_recv())
            return
        pl.when(jnp.logical_and(hears_from(ahead), ahead != 0))(
            lambda: move(number, ahead, start, count, to).wait_recv()
        )
        pl.when(ahead == 0)(lambda: own_move(start, count, to).wait())

    def retire(number, ahead, start, count, to):
        if isinstance(ahead, int):
            pl.when(sends_to(ahead))(lambda: move(number, ahead, start, count, to).wait_send())
            return
        pl.when(jnp.logical_and(sends_to(ahead), ahead != 0))(
            lambda: move(number, ahead, start, count, to).wait_send()
        )

    def all_moves(act):
        @pl.when(odd == 0)
        def _():
            run_moves(even_moves, act)

        @pl.when(odd == 1)
        def _():
            run_moves(odd_moves, act)

        run_moves(left_moves, act)

    all_moves(begin)
    for number, ahead, start, to in embed_moves:
        ok = jnp.logical_and(g - ahead >= 0, g - ahead < N_OFF)
        pl.when(ok)(lambda n=number, a=ahead, s=start, t=to: embed_move(n, a, s, t).start())

    copies[2].wait()
    lane = lax.broadcasted_iota(jnp.int32, (64, 128), 1)
    row64 = lax.broadcasted_iota(jnp.int32, (64, 128), 0)
    twice = jnp.where(lane % 64 == row64, 1.0, 0.0).astype(BF16)
    low = lane < 64
    taps = dot(wfilt[...], twice)

    def tap_of(layer, p, q):
        start = ((layer * 3 + p) * 3 + q) * 64
        return taps[start : start + 64]

    none = jnp.zeros((64, 128), F32)
    for jin in range(4):
        for jout in range(2):
            for kout in range(2):
                q = jin - jout
                base = (jout * 2 + kout) * 64
                rows = pl.ds(base, 64)
                if q < 0 or q > 2:
                    halves = (none, none)
                elif kout == 0:
                    halves = (jnp.where(low, tap_of(0, 0, q), tap_of(0, 1, q)), jnp.where(low, tap_of(0, 2, q), none))
                else:
                    halves = (jnp.where(low, none, tap_of(0, 0, q)), jnp.where(low, tap_of(0, 1, q), tap_of(0, 2, q)))
                first[jin, rows, 0:128] = halves[0].astype(BF16)
                first[jin, rows, 128:256] = halves[1].astype(BF16)

    head_row = head[0:1, :]
    h0 = head_row.astype(BF16).astype(F32)
    h1 = (head_row - h0).astype(BF16).astype(F32)
    h2 = (head_row - h0 - h1).astype(BF16).astype(F32)
    row8 = lax.broadcasted_iota(jnp.int32, (8, 64), 0)
    head8 = jnp.where(row8 == 0, h0, jnp.where(row8 == 1, h1, jnp.where(row8 == 2, h2, 0.0))).astype(BF16)
    head_twice = jnp.sum(dot(head8, twice), axis=0, keepdims=True)
    row96 = lax.broadcasted_iota(jnp.int32, (96, 128), 0)
    lane96 = lax.broadcasted_iota(jnp.int32, (96, 128), 1)
    k_out = row96 % 16
    kp = lane96 // 64
    q_of = row96 // 32

    def hi_lo(value):
        hi = value.astype(BF16).astype(F32)
        return hi, (value - hi).astype(BF16).astype(F32)

    folded = []
    for p in range(3):
        pieces = []
        for q in range(3):
            whole = jnp.sum(dot(head8, tap_of(1, p, q).astype(BF16)), axis=0, keepdims=True)
            for part in hi_lo(whole):
                pieces.append(jnp.broadcast_to(part, (16, 128)))
        folded.append(jnp.concatenate(pieces, axis=0))
    for m in range(9):
        p_of = 2 * m + kp - k_out
        block = jnp.zeros((96, 128), F32)
        for p in range(3):
            block = jnp.where(p_of == p, folded[p], block)
        gin[:, m * 128 : (m + 1) * 128] = block.astype(BF16)
    head_hi, head_lo = hi_lo(head_twice)
    head_block = jnp.where(row96 % 32 < 16, head_hi, head_lo)
    for m in range(8):
        block = jnp.where(jnp.logical_and(q_of == 1, 2 * m + kp == k_out), head_block, 0.0)
        gpair[:, m * 128 : (m + 1) * 128] = block.astype(BF16)

    for copy in copies[:2] + copies[3:]:
        copy.wait()
    for number, ahead, start, to in embed_moves:
        ok = jnp.logical_and(g + ahead >= 0, g + ahead < N_OFF)
        pl.when(ok)(lambda n=number, a=ahead, s=start, t=to: embed_move(n, a, s, t).wait_recv())
    erow = lax.broadcasted_iota(jnp.int32, (96, 64), 0) + 64 * g - 16
    e_in = jnp.logical_and(erow >= 0, erow < BAND)
    e_val = jnp.where(e_in, ewin[...].astype(F32), 0.0).astype(BF16)
    e_two = dot(e_val, twice)
    e_two = jnp.where(lane96 < 64, e_two, pltpu.roll(e_two, 92, 0)).astype(BF16)
    ee[...] = dot(vsel_e[...], e_two).reshape(10, 16, 128)

    all_moves(finish)
    row = lax.broadcasted_iota(jnp.int32, (ROWS, 1), 0)
    bin_of = 128 * d - 32 + jnp.where(row < W_LEFT, row, row - W_LEFT + 64 * g)
    inside = jnp.logical_and(bin_of >= 0, bin_of < BINS)
    x = jnp.where(inside, win[...].astype(F32), 0.0)
    for layer, spread in ((0, 4), (1, 8)):
        y = dot(jnp.maximum(x, 0.0).astype(BF16), wconv[layer])
        c = pltpu.roll(y[:, 0:128], spread, 0) + y[:, 128:256] + pltpu.roll(y[:, 256:384], ROWS - spread, 0)
        v = jnp.maximum(c, 0.0).astype(BF16)
        x = jnp.where(inside, (x + dot(v, wout[layer])).astype(BF16).astype(F32), 0.0)
    projected = dot(x.astype(BF16), wproj[...]).astype(BF16).astype(F32)
    projected = jnp.where(inside, projected, 0.0)
    swapped = pltpu.roll(projected, 64, 1)
    lane_r = lax.broadcasted_iota(jnp.int32, (W_RIGHT, 128), 1) < 64
    lane_l = lax.broadcasted_iota(jnp.int32, (W_LEFT, 128), 1) < 64
    left = jnp.where(lane_l, projected[:W_LEFT], swapped[:W_LEFT]).astype(BF16)
    ahead4 = pltpu.roll(projected[W_LEFT:], W_RIGHT - 4, 0)
    right = jnp.where(lane_r, swapped[W_LEFT:], ahead4).astype(BF16)
    ll[...] = dot(vsel_l[...], left).reshape(2, 288, 128)
    rr[...] = dot(vsel_r[...], right).reshape(2, 432, 128)

    def build(m, carry):
        e = jnp.broadcast_to(ee[m][None], (18, 16, 128)).reshape(288, 128)
        for par in range(2):
            value = rr[par, pl.ds(pl.multiple_of(m * 16, 16), 288), :] + ll[par] + e
            pair[par, :, pl.ds(pl.multiple_of(m * 128, 128), 128)] = jnp.maximum(value, 0.0).astype(BF16)
        return carry

    lax.fori_loop(0, 10, build, 0)

    @pl.when(d == 0)
    def _():
        pair[:, 0:16, :] = jnp.zeros((2, 16, 1280), BF16)

    @pl.when(d == N_DIAG - 1)
    def _():
        pair[:, 272:288, :] = jnp.zeros((2, 16, 1280), BF16)

    @pl.when(g == 0)
    def _():
        pair[:, :, 0:128] = jnp.zeros((2, 288, 128), BF16)

    @pl.when(g == N_OFF - 1)
    def _():
        pair[:, :, 1152:1280] = jnp.zeros((2, 288, 128), BF16)

    def convolve(m, carry):
        cols = pl.ds(pl.multiple_of(m * 128, 128), 256)
        acc = dot_nt(pair[0, 0:272, cols], first[0])
        acc = acc + dot_nt(pair[1, 0:272, cols], first[1])
        acc = acc + dot_nt(pair[0, 16:288, cols], first[2])
        acc = acc + dot_nt(pair[1, 16:288, cols], first[3])
        acc = jnp.maximum(acc, 0.0).astype(BF16)
        out_cols = pl.ds(pl.multiple_of(m * 128, 128), 128)
        inner[0, :, out_cols] = acc[:, 0:128]
        inner[1, :, out_cols] = acc[:, 128:256]
        return carry

    lax.fori_loop(0, 9, convolve, 0)

    @pl.when(d == 0)
    def _():
        inner[0, 0:16, :] = jnp.zeros((16, 1152), BF16)

    @pl.when(d == N_DIAG - 1)
    def _():
        inner[1, 256:272, :] = jnp.zeros((16, 1152), BF16)

    lane272 = lax.broadcasted_iota(jnp.int32, (272, 128), 1)

    @pl.when(g == 0)
    def _():
        for par in range(2):
            inner[par, :, 0:128] = jnp.where(lane272 < 64, 0.0, inner[par, :, 0:128].astype(F32)).astype(BF16)

    @pl.when(g == N_OFF - 1)
    def _():
        for par in range(2):
            edge = inner[par, :, 1024:1152].astype(F32)
            inner[par, :, 1024:1152] = jnp.where(lane272 < 64, edge, 0.0).astype(BF16)

    def turned(value):
        full = jnp.concatenate([value, jnp.zeros((256, 32), F32)], axis=1)
        return jnp.transpose(full)

    sums = []
    for par in range(2):
        t = dot_nt(inner[par], gin[...])
        t = t + dot_nt(pair[1 - par, 16 * par : 16 * par + 272, 128:1152], gpair[...])
        sums.append((turned(t[0:256]), turned(t[16:272])))

    def both(value, q):
        return value[32 * q : 32 * q + 16] + value[32 * q + 16 : 32 * q + 32]

    (a0, a1), (b0, b1) = sums
    even = both(a0, 0) + both(b0, 1) + both(a1, 2)
    odds = both(b0, 0) + both(a1, 1) + both(b1, 2)
    flat = jnp.concatenate([even, odds], axis=1)
    p0 = flat.astype(BF16).astype(F32)
    p1 = (flat - p0).astype(BF16).astype(F32)
    p2 = flat - p0 - p1
    stacked = jnp.concatenate([p0, p1, p2], axis=0).astype(BF16)
    placed = dot(stacked, vsel_b[...])
    placed = placed[0:16] + placed[16:32] + placed[32:48]
    for r in range(4):
        pred[pl.ds(r, 16, stride=4), :] = placed[:, r * 128 : (r + 1) * 128]

    o_of = lax.broadcasted_iota(jnp.int32, (64, 128), 0) + 64 * g
    i_of = lax.broadcasted_iota(jnp.int32, (64, 128), 1) + 128 * d
    valid = jnp.where(o_of + i_of < BINS, vmask[...].astype(F32), 0.0)
    err = valid * (pred[...] - vtarget[...]) ** 2
    red1[t1] = jnp.sum(err.reshape(8, 8, 128), axis=0)

    def reduce_copy(buf, slot, peer, send, recv, wait_slot):
        return pltpu.make_async_remote_copy(
            src_ref=buf.at[slot], dst_ref=buf.at[slot], send_sem=send, recv_sem=recv.at[wait_slot],
            device_id=peer, device_id_type=pl.DeviceIdType.MESH,
        )

    def reduce_over(buf, mine, peer, send, recv):
        def go(k, carry):
            t, where = peer(k)
            reduce_copy(buf, mine, where, send.at[k], recv, mine).start()
            return carry

        def arrived(k, carry):
            t, where = peer(k)
            reduce_copy(buf, t, where, send.at[k], recv, t).wait_recv()
            return carry

        lax.fori_loop(1, 16, go, 0)
        lax.fori_loop(1, 16, arrived, 0)
        return jnp.sum(buf[...], axis=0)

    def reduce_retire(buf, mine, peer, send, recv):
        def sent(k, carry):
            t, where = peer(k)
            reduce_copy(buf, mine, where, send.at[k], recv, mine).wait_send()
            return carry

        lax.fori_loop(1, 16, sent, 0)

    red2[t2] = reduce_over(red1, t1, peer1, s1, r1)
    total_err = reduce_over(red2, t2, peer2, s2, r2)
    loss[0, 0] = jnp.sum(total_err) / (BAND * BINS)

    all_moves(retire)
    for number, ahead, start, to in embed_moves:
        ok = jnp.logical_and(g - ahead >= 0, g - ahead < N_OFF)
        pl.when(ok)(lambda n=number, a=ahead, s=start, t=to: embed_move(n, a, s, t).wait_send())
    reduce_retire(red1, t1, peer1, s1, r1)
    reduce_retire(red2, t2, peer2, s2, r2)


def body(features, conv_weight, out_weight, proj_weight, offset_embed, pair_filter_weight, head_weight, target, cell_mask):
    anywhere = pl.BlockSpec(memory_space=pl.ANY)
    vmem = pl.BlockSpec(memory_space=pltpu.VMEM)
    picks = [jnp.asarray(value) for value in selections()]
    pred, loss = pl.pallas_call(
        kernel,
        out_shape=(jax.ShapeDtypeStruct((64, 128), F32), jax.ShapeDtypeStruct((1, 1), F32)),
        in_specs=[anywhere] * 6 + [vmem] + [anywhere] * 6,
        out_specs=(vmem, pl.BlockSpec(memory_space=pltpu.SMEM)),
        scratch_shapes=[
            pltpu.VMEM((ROWS, D), BF16),
            pltpu.VMEM((96, CP), BF16),
            pltpu.VMEM((2, D, 384), BF16),
            pltpu.VMEM((2, 128, D), BF16),
            pltpu.VMEM((D, 128), BF16),
            pltpu.VMEM((1152, CP), BF16),
            pltpu.VMEM((64, 128), F32),
            pltpu.VMEM((64, 128), jnp.int32),
            pltpu.VMEM((864, W_RIGHT), BF16),
            pltpu.VMEM((576, W_LEFT), BF16),
            pltpu.VMEM((160, 96), BF16),
            pltpu.VMEM((512, 512), BF16),
            pltpu.VMEM((4, 256, 256), BF16),
            pltpu.VMEM((96, 1152), BF16),
            pltpu.VMEM((96, 1024), BF16),
            pltpu.VMEM((2, 432, 128), F32),
            pltpu.VMEM((2, 288, 128), F32),
            pltpu.VMEM((10, 16, 128), F32),
            pltpu.VMEM((2, 288, 1280), BF16),
            pltpu.VMEM((2, 272, 1152), BF16),
            pltpu.VMEM((16, 8, 128), F32),
            pltpu.VMEM((16, 8, 128), F32),
            pltpu.SemaphoreType.DMA((17,)),
            pltpu.SemaphoreType.DMA((7,)),
            pltpu.SemaphoreType.DMA((7,)),
            pltpu.SemaphoreType.DMA,
            pltpu.SemaphoreType.DMA((16,)),
            pltpu.SemaphoreType.DMA((16,)),
            pltpu.SemaphoreType.DMA((16,)),
            pltpu.SemaphoreType.DMA((16,)),
        ],
        compiler_params=pltpu.CompilerParams(
            collective_id=0, has_side_effects=True, vmem_limit_bytes=40 * 1024 * 1024
        ),
        name="contact_block",
    )(
        features, conv_weight, out_weight, proj_weight, offset_embed,
        pair_filter_weight.reshape(1152, CP), head_weight.reshape(1, CP), target, cell_mask, *picks,
    )
    return pred, loss[0, 0]


def solution(mesh):
    in_specs = (P("diag", None), P(), P(), P(), P("off", None), P(), P(), P("off", "diag"), P("off", "diag"))
    out_specs = (P("off", "diag"), P())
    return jax.shard_map(body, mesh=mesh, in_specs=in_specs, out_specs=out_specs, check_vma=False)
```

```python
import jax
import jax.numpy as jnp
import ml_dtypes
import numpy as np
from jax import lax
from jax.experimental import pallas as pl
from jax.experimental.pallas import tpu as pltpu
from jax.sharding import PartitionSpec as P

BINS = 4096
BAND = 512
CP = 64
D = 256
N_DIAG = 32
N_OFF = 8
ROWS = 192
W_RIGHT = 256
F32 = jnp.float32
BF16 = jnp.bfloat16
NT = (((1,), (1,)), ((), ()))


def selections():
    def one_hot(index, width):
        index = np.asarray(index).reshape(-1)
        return (index[:, None] == np.arange(width)[None, :]).astype(ml_dtypes.bfloat16)

    par, v, r, s = np.meshgrid(np.arange(2), np.arange(27), np.arange(4), np.arange(4), indexing="ij")
    right = one_hot(4 * (2 * v + par) + r + s + 16, W_RIGHT)
    par, jj, r, s = np.meshgrid(np.arange(2), np.arange(18), np.arange(4), np.arange(4), indexing="ij")
    left = one_hot(4 * (2 * jj + par) + s + 24, ROWS)
    m, r, s = np.meshgrid(np.arange(10), np.arange(4), np.arange(4), indexing="ij")
    embed = one_hot(8 * m + r + 8, 96)
    jo, jj, r, s = np.meshgrid(np.arange(2), np.arange(16), np.arange(4), np.arange(4), indexing="ij")
    back = one_hot(r * 128 + 4 * (2 * jj + jo) + s, 512)
    return right, left, embed, back


def dot(a, b):
    return jnp.dot(a, b, preferred_element_type=F32)


def dot_nt(a, b):
    return lax.dot_general(a, b, NT, preferred_element_type=F32)


def kernel(
    feat, conv, outw, proj, emb, filt, head, target, mask, sel_r, sel_l, sel_e, sel_b,
    pred, loss,
    vhead, win, ewin, wconv, wout, wproj, wfilt, vtarget, vmask, vsel_r, vsel_l, vsel_e, vsel_b, vpred,
    rwin, first, gin, gpair, rr, ll, ee, pair, inner, red1, red2,
    local_sem, send_sem, recv_sem, pred_sem, s1, r1, s2, r2, vloss, loss_sem,
):
    d = lax.axis_index("diag")
    g = lax.axis_index("off")
    h = g // 2
    odd = g % 2
    core = odd
    z_lo = d // 16
    xy = d % 16
    x_at = xy // 4
    y_at = xy % 4
    z_at = 2 * h + z_lo

    feat_moves = [(0, -1, 96, 0), (1, 1, 0, 160)]
    embed_moves = [(2, -1, 48, 0), (3, 1, 0, 80)]
    even_moves = [(4, h - 1, 96, 32, 0), (5, h, 0, 128, 32), (6, h + 1, 0, 96, 160)]
    odd_moves = [(4, h, 32, 96, 0), (5, h + 1, 0, 128, 96), (6, h + 2, 0, 32, 224)]

    def on_diag(index):
        return jnp.logical_and(index >= 0, index < N_DIAG)

    def on_off(index):
        return jnp.logical_and(index >= 0, index < N_OFF)

    def remote(src, dst, number, peer):
        return pltpu.make_async_remote_copy(
            src_ref=src, dst_ref=dst, send_sem=send_sem.at[number], recv_sem=recv_sem.at[number],
            device_id=peer, device_id_type=pl.DeviceIdType.MESH,
        )

    def feat_move(number, ahead, start, to):
        return remote(win.at[pl.ds(32 + start, 32)], win.at[pl.ds(to, 32)], number, (d - ahead, g))

    def embed_move(number, ahead, start, to):
        return remote(ewin.at[pl.ds(16 + start, 16)], ewin.at[pl.ds(to, 16)], number, (d, g - ahead))

    def right_move(number, ahead, start, count, to):
        return remote(win.at[pl.ds(32 + start, count)], rwin.at[pl.ds(to, count)], number, (d - ahead, g))

    def each_right(act):
        pl.when(odd == 0)(lambda: [act(*one) for one in even_moves] and None)
        pl.when(odd == 1)(lambda: [act(*one) for one in odd_moves] and None)

    def wrapped(value, size):
        return jnp.where(value >= size, value - size, value)

    def far(step, size):
        return min(step, size - step)

    z_steps = sorted(((a, b) for a in range(8) for b in range(2) if a or b), key=lambda t: -far(t[0], 8) * 2 - t[1])
    xy_steps = sorted(((a, b) for a in range(4) for b in range(4) if a or b), key=lambda t: -far(t[0], 4) - far(t[1], 4))

    def z_peer(step):
        z = wrapped(z_at + step[0], 8)
        c = wrapped(core + step[1], 2)
        return (z % 2 * 16 + xy, z // 2 * 2 + c)

    def xy_peer(step):
        return (z_lo * 16 + wrapped(x_at + step[0], 4) * 4 + wrapped(y_at + step[1], 4), g)

    z_slot = z_at * 2 + core
    xy_slot = xy

    own = [
        pltpu.make_async_copy(feat, win.at[pl.ds(32, 128)], local_sem.at[16]),
        pltpu.make_async_copy(emb, ewin.at[pl.ds(16, 64)], local_sem.at[17]),
    ]
    for copy in own:
        copy.start()
    barrier = pltpu.get_barrier_semaphore()

    def greet(peer, times=1):
        pl.semaphore_signal(barrier, inc=times, device_id=peer, device_id_type=pl.DeviceIdType.MESH)

    def count_of(cond):
        return jnp.where(cond, 1, 0).astype(jnp.int32)

    total = jnp.int32(30)
    for reach in (-1, 1):
        ok = on_diag(d - reach)
        pl.when(ok)(lambda reach=reach: greet((d - reach, g)))
        total = total + count_of(ok)
        ok = on_off(g - reach)
        pl.when(ok)(lambda reach=reach: greet((d, g - reach)))
        total = total + count_of(ok)
    for step in range(3):
        ahead = h - 1 + odd + step
        ok_s = jnp.logical_and(on_diag(d - ahead), ahead != 0)
        ok_r = jnp.logical_and(on_diag(d + ahead), ahead != 0)
        pl.when(ok_s)(lambda ahead=ahead: greet((d - ahead, g)))
        pl.when(ok_r)(lambda ahead=ahead: greet((d + ahead, g)))
        total = total + count_of(ok_s) + count_of(ok_r)
    for step in z_steps:
        greet(z_peer(step))
    for step in xy_steps:
        greet(xy_peer(step))

    def right_begin(number, ahead, start, count, to):
        pl.when(jnp.logical_and(on_diag(d - ahead), ahead != 0))(
            lambda: right_move(number, ahead, start, count, to).start()
        )

    for copy in own:
        copy.wait()
    pl.semaphore_wait(barrier, total)
    each_right(right_begin)
    for one in feat_moves:
        pl.when(on_diag(d - one[1]))(lambda one=one: feat_move(*one).start())
    for one in embed_moves:
        pl.when(on_off(g - one[1]))(lambda one=one: embed_move(*one).start())

    loads = [(filt, wfilt), (head, vhead)]
    for layer in range(2):
        for tap in range(3):
            loads.append((conv.at[layer, tap], wconv.at[layer, :, pl.ds(128 * tap, 128)]))
    loads += [(outw, wout), (proj, wproj), (sel_l, vsel_l), (sel_e, vsel_e)]
    loads += [(sel_r, vsel_r), (sel_b, vsel_b), (target, vtarget), (mask, vmask)]
    copies = [pltpu.make_async_copy(a, b, local_sem.at[i]) for i, (a, b) in enumerate(loads)]
    for copy in copies:
        copy.start()

    copies[0].wait()
    copies[1].wait()
    lane = lax.broadcasted_iota(jnp.int32, (64, 128), 1)
    row64 = lax.broadcasted_iota(jnp.int32, (64, 128), 0)
    twice = jnp.where(lane % 64 == row64, 1.0, 0.0).astype(BF16)
    low = lane < 64
    taps = dot(wfilt[...], twice)

    def tap_of(layer, p, q):
        start = ((layer * 3 + p) * 3 + q) * 64
        return taps[start : start + 64]

    none = jnp.zeros((64, 128), F32)
    for jin in range(4):
        for jout in range(2):
            for kout in range(2):
                q = jin - jout
                base = (jout * 2 + kout) * 64
                rows = pl.ds(base, 64)
                if q < 0 or q > 2:
                    halves = (none, none)
                elif kout == 0:
                    halves = (jnp.where(low, tap_of(0, 0, q), tap_of(0, 1, q)), jnp.where(low, tap_of(0, 2, q), none))
                else:
                    halves = (jnp.where(low, none, tap_of(0, 0, q)), jnp.where(low, tap_of(0, 1, q), tap_of(0, 2, q)))
                first[rows, jin * 256 : jin * 256 + 128] = halves[0].astype(BF16)
                first[rows, jin * 256 + 128 : jin * 256 + 256] = halves[1].astype(BF16)

    head_row = vhead[0:1, :]
    h0 = head_row.astype(BF16).astype(F32)
    h1 = (head_row - h0).astype(BF16).astype(F32)
    h2 = (head_row - h0 - h1).astype(BF16).astype(F32)
    row8 = lax.broadcasted_iota(jnp.int32, (8, 64), 0)
    head8 = jnp.where(row8 == 0, h0, jnp.where(row8 == 1, h1, jnp.where(row8 == 2, h2, 0.0))).astype(BF16)
    head_twice = jnp.sum(dot(head8, twice), axis=0, keepdims=True)
    row96 = lax.broadcasted_iota(jnp.int32, (96, 128), 0)
    lane96 = lax.broadcasted_iota(jnp.int32, (96, 128), 1)
    k_out = row96 % 16
    kp = lane96 // 64
    q_of = row96 // 32

    def hi_lo(value):
        hi = value.astype(BF16).astype(F32)
        return hi, (value - hi).astype(BF16).astype(F32)

    folded = []
    for p in range(3):
        pieces = []
        for q in range(3):
            whole = jnp.sum(dot(head8, tap_of(1, p, q).astype(BF16)), axis=0, keepdims=True)
            for part in hi_lo(whole):
                pieces.append(jnp.broadcast_to(part, (16, 128)))
        folded.append(jnp.concatenate(pieces, axis=0))
    for m in range(9):
        p_of = 2 * m + kp - k_out
        block = jnp.zeros((96, 128), F32)
        for p in range(3):
            block = jnp.where(p_of == p, folded[p], block)
        gin[:, m * 128 : (m + 1) * 128] = block.astype(BF16)
    head_hi, head_lo = hi_lo(head_twice)
    head_block = jnp.where(row96 % 32 < 16, head_hi, head_lo)
    for m in range(8):
        block = jnp.where(jnp.logical_and(q_of == 1, 2 * m + kp == k_out), head_block, 0.0)
        gpair[:, m * 128 : (m + 1) * 128] = block.astype(BF16)

    for copy in copies[2:10]:
        copy.wait()
    for one in feat_moves:
        pl.when(on_diag(d + one[1]))(lambda one=one: feat_move(*one).wait_recv())

    def trunk(window, rows, start):
        at = lax.broadcasted_iota(jnp.int32, (rows, 1), 0) + start
        inside = jnp.logical_and(at >= 0, at < BINS)
        x = jnp.where(inside, window[...].astype(F32), 0.0)
        for layer, spread in ((0, 4), (1, 8)):
            y = dot(jnp.maximum(x, 0.0).astype(BF16), wconv[layer])
            c = pltpu.roll(y[:, 0:128], spread, 0) + y[:, 128:256] + pltpu.roll(y[:, 256:384], rows - spread, 0)
            v = jnp.maximum(c, 0.0).astype(BF16)
            x = jnp.where(inside, (x + dot(v, wout[layer])).astype(BF16).astype(F32), 0.0)
        value = dot(x.astype(BF16), wproj[...]).astype(BF16).astype(F32)
        return value, pltpu.roll(value, 64, 1)

    projected, swapped = trunk(win, ROWS, 128 * d - 32)

    for copy in copies[10:]:
        copy.wait()
    lane_l = lax.broadcasted_iota(jnp.int32, (ROWS, 128), 1) < 64
    left = jnp.where(lane_l, projected, swapped).astype(BF16)
    ll[...] = dot(vsel_l[...], left).reshape(2, 288, 128)
    for one in embed_moves:
        pl.when(on_off(g + one[1]))(lambda one=one: embed_move(*one).wait_recv())
    erow = lax.broadcasted_iota(jnp.int32, (96, 64), 0) + 64 * g - 16
    e_in = jnp.logical_and(erow >= 0, erow < BAND)
    e_val = jnp.where(e_in, ewin[...].astype(F32), 0.0).astype(BF16)
    e_two = dot(e_val, twice)
    e_two = jnp.where(lane96 < 64, e_two, pltpu.roll(e_two, 92, 0)).astype(BF16)
    ee[...] = dot(vsel_e[...], e_two).reshape(10, 16, 128)

    def right_finish(number, ahead, start, count, to):
        pl.when(jnp.logical_and(on_diag(d + ahead), ahead != 0))(
            lambda: right_move(number, ahead, start, count, to).wait_recv()
        )

    each_right(right_finish)

    def right_own(number, ahead, start, count, to):
        @pl.when(ahead == 0)
        def _():
            rwin[to : to + count, :] = win[32 + start : 32 + start + count, :]

    each_right(right_own)
    projected, swapped = trunk(rwin, W_RIGHT, 128 * d + 64 * g - 32)
    lane_r = lax.broadcasted_iota(jnp.int32, (W_RIGHT, 128), 1) < 64
    right = jnp.where(lane_r, swapped, pltpu.roll(projected, W_RIGHT - 4, 0)).astype(BF16)
    rr[...] = dot(vsel_r[...], right).reshape(2, 432, 128)

    for m in range(10):
        e = jnp.broadcast_to(ee[m][None], (18, 16, 128)).reshape(288, 128)
        for par in range(2):
            value = rr[par, m * 16 : m * 16 + 288, :] + ll[par] + e
            pair[par, :, m * 128 : (m + 1) * 128] = jnp.maximum(value, 0.0).astype(BF16)

    @pl.when(d == 0)
    def _():
        pair[:, 0:16, :] = jnp.zeros((2, 16, 1280), BF16)

    @pl.when(d == N_DIAG - 1)
    def _():
        pair[:, 272:288, :] = jnp.zeros((2, 16, 1280), BF16)

    @pl.when(g == 0)
    def _():
        pair[:, :, 0:128] = jnp.zeros((2, 288, 128), BF16)

    @pl.when(g == N_OFF - 1)
    def _():
        pair[:, :, 1152:1280] = jnp.zeros((2, 288, 128), BF16)

    for m in range(9):
        cols = slice(m * 128, m * 128 + 256)
        near = jnp.concatenate(
            [pair[0, 0:272, cols], pair[1, 0:272, cols], pair[0, 16:288, cols], pair[1, 16:288, cols]], axis=1
        )
        acc = jnp.maximum(dot_nt(near, first[...]), 0.0).astype(BF16)
        inner[0, :, m * 128 : (m + 1) * 128] = acc[:, 0:128]
        inner[1, :, m * 128 : (m + 1) * 128] = acc[:, 128:256]

    @pl.when(d == 0)
    def _():
        inner[0, 0:16, :] = jnp.zeros((16, 1152), BF16)

    @pl.when(d == N_DIAG - 1)
    def _():
        inner[1, 256:272, :] = jnp.zeros((16, 1152), BF16)

    lane272 = lax.broadcasted_iota(jnp.int32, (272, 128), 1)

    @pl.when(g == 0)
    def _():
        for par in range(2):
            inner[par, :, 0:128] = jnp.where(lane272 < 64, 0.0, inner[par, :, 0:128].astype(F32)).astype(BF16)

    @pl.when(g == N_OFF - 1)
    def _():
        for par in range(2):
            edge = inner[par, :, 1024:1152].astype(F32)
            inner[par, :, 1024:1152] = jnp.where(lane272 < 64, edge, 0.0).astype(BF16)

    def turned(value):
        full = jnp.concatenate([value, jnp.zeros((256, 32), F32)], axis=1)
        return jnp.transpose(full)

    sums = []
    for par in range(2):
        t = dot_nt(inner[par], gin[...])
        t = t + dot_nt(pair[1 - par, 16 * par : 16 * par + 272, 128:1152], gpair[...])
        sums.append((turned(t[0:256]), turned(t[16:272])))

    def both(value, q):
        return value[32 * q : 32 * q + 16] + value[32 * q + 16 : 32 * q + 32]

    (a0, a1), (b0, b1) = sums
    even = both(a0, 0) + both(b0, 1) + both(a1, 2)
    odds = both(b0, 0) + both(a1, 1) + both(b1, 2)
    flat = jnp.concatenate([even, odds], axis=1)
    p0 = flat.astype(BF16).astype(F32)
    p1 = (flat - p0).astype(BF16).astype(F32)
    p2 = flat - p0 - p1
    stacked = jnp.concatenate([p0, p1, p2], axis=0).astype(BF16)
    placed = dot(stacked, vsel_b[...])
    placed = placed[0:16] + placed[16:32] + placed[32:48]
    for r in range(4):
        vpred[pl.ds(r, 16, stride=4), :] = placed[:, r * 128 : (r + 1) * 128]
    out_copy = pltpu.make_async_copy(vpred, pred, pred_sem)
    out_copy.start()

    o_of = lax.broadcasted_iota(jnp.int32, (64, 128), 0) + 64 * g
    i_of = lax.broadcasted_iota(jnp.int32, (64, 128), 1) + 128 * d
    valid = jnp.where(o_of + i_of < BINS, vmask[...].astype(F32), 0.0)
    err = valid * (vpred[...] - vtarget[...]) ** 2

    def reduce_over(buf, slot, value, steps, peer, send, recv):
        buf[slot] = value
        for step in steps:
            pltpu.make_async_remote_copy(
                src_ref=buf.at[slot], dst_ref=buf.at[slot], send_sem=send, recv_sem=recv,
                device_id=peer(step), device_id_type=pl.DeviceIdType.MESH,
            ).start()
        pltpu.make_async_copy(buf.at[pl.ds(0, 15)], buf.at[pl.ds(0, 15)], recv).wait()
        return jnp.sum(buf[...], axis=0)

    def reduce_retire(buf, send):
        pltpu.make_async_copy(buf.at[pl.ds(0, 15)], buf.at[pl.ds(0, 15)], send).wait()

    partial = jnp.sum(err.reshape(8, 8, 128), axis=0)
    partial = reduce_over(red1, z_slot, partial, z_steps, z_peer, s1, r1)
    partial = reduce_over(red2, xy_slot, partial, xy_steps, xy_peer, s2, r2)
    vloss[...] = partial
    loss_copy = pltpu.make_async_copy(vloss, loss, loss_sem)
    loss_copy.start()

    out_copy.wait()
    loss_copy.wait()
    for one in feat_moves:
        pl.when(on_diag(d - one[1]))(lambda one=one: feat_move(*one).wait_send())
    for one in embed_moves:
        pl.when(on_off(g - one[1]))(lambda one=one: embed_move(*one).wait_send())

    def right_retire(number, ahead, start, count, to):
        pl.when(jnp.logical_and(on_diag(d - ahead), ahead != 0))(
            lambda: right_move(number, ahead, start, count, to).wait_send()
        )

    each_right(right_retire)
    reduce_retire(red1, s1)
    reduce_retire(red2, s2)


def finish(pred_in, parts, pred, loss):
    pred[...] = pred_in[...]
    loss[0, 0] = jnp.sum(parts[...]) / (BAND * BINS)


def body(features, conv_weight, out_weight, proj_weight, offset_embed, pair_filter_weight, head_weight, target, cell_mask):
    vmem = pl.BlockSpec(memory_space=pltpu.VMEM)
    anywhere = pl.BlockSpec(memory_space=pltpu.HBM)
    picks = [jnp.asarray(value) for value in selections()]
    pred, loss = pl.pallas_call(
        kernel,
        out_shape=(jax.ShapeDtypeStruct((64, 128), F32), jax.ShapeDtypeStruct((8, 128), F32)),
        in_specs=[anywhere] * 13,
        out_specs=(anywhere, anywhere),
        scratch_shapes=[
            pltpu.VMEM((1, CP), F32),
            pltpu.VMEM((ROWS, D), BF16),
            pltpu.VMEM((96, CP), BF16),
            pltpu.VMEM((2, D, 384), BF16),
            pltpu.VMEM((2, 128, D), BF16),
            pltpu.VMEM((D, 128), BF16),
            pltpu.VMEM((1152, CP), BF16),
            pltpu.VMEM((64, 128), F32),
            pltpu.VMEM((64, 128), jnp.int32),
            pltpu.VMEM((864, W_RIGHT), BF16),
            pltpu.VMEM((576, ROWS), BF16),
            pltpu.VMEM((160, 96), BF16),
            pltpu.VMEM((512, 512), BF16),
            pltpu.VMEM((64, 128), F32),
            pltpu.VMEM((W_RIGHT, D), BF16),
            pltpu.VMEM((256, 1024), BF16),
            pltpu.VMEM((96, 1152), BF16),
            pltpu.VMEM((96, 1024), BF16),
            pltpu.VMEM((2, 432, 128), F32),
            pltpu.VMEM((2, 288, 128), F32),
            pltpu.VMEM((10, 16, 128), F32),
            pltpu.VMEM((2, 288, 1280), BF16),
            pltpu.VMEM((2, 272, 1152), BF16),
            pltpu.VMEM((16, 8, 128), F32),
            pltpu.VMEM((16, 8, 128), F32),
            pltpu.SemaphoreType.DMA((18,)),
            pltpu.SemaphoreType.DMA((7,)),
            pltpu.SemaphoreType.DMA((7,)),
            pltpu.SemaphoreType.DMA,
            pltpu.SemaphoreType.DMA,
            pltpu.SemaphoreType.DMA,
            pltpu.SemaphoreType.DMA,
            pltpu.SemaphoreType.DMA,
            pltpu.VMEM((8, 128), F32),
            pltpu.SemaphoreType.DMA,
        ],
        compiler_params=pltpu.CompilerParams(
            collective_id=0, has_side_effects=True, vmem_limit_bytes=64 * 1024 * 1024
        ),
        name="contact_block",
    )(
        features, conv_weight, out_weight, proj_weight, offset_embed,
        pair_filter_weight.reshape(1152, CP), head_weight.reshape(1, CP), target, cell_mask, *picks,
    )
    pred, loss = pl.pallas_call(
        finish,
        out_shape=(jax.ShapeDtypeStruct((64, 128), F32), jax.ShapeDtypeStruct((1, 1), F32)),
        in_specs=[vmem, vmem],
        out_specs=(vmem, pl.BlockSpec(memory_space=pltpu.SMEM)),
        compiler_params=pltpu.CompilerParams(vmem_limit_bytes=64 * 1024 * 1024),
        name="finish",
    )(pred, loss)
    return pred, loss[0, 0]


def solution(mesh):
    in_specs = (P("diag", None), P(), P(), P(), P("off", None), P(), P(), P("off", "diag"), P("off", "diag"))
    out_specs = (P("off", "diag"), P())
    return jax.shard_map(body, mesh=mesh, in_specs=in_specs, out_specs=out_specs, check_vma=False)
```

```python
import jax
import jax.numpy as jnp
import ml_dtypes
import numpy as np
from jax import lax
from jax.experimental import pallas as pl
from jax.experimental.pallas import tpu as pltpu
from jax.sharding import PartitionSpec as P

BINS = 4096
BAND = 512
CP = 64
D = 256
N_DIAG = 32
N_OFF = 8
ROWS = 192
W_RIGHT = 256
F32 = jnp.float32
BF16 = jnp.bfloat16
NT = (((1,), (1,)), ((), ()))


def selections():
    def one_hot(index, width):
        index = np.asarray(index).reshape(-1)
        return (index[:, None] == np.arange(width)[None, :]).astype(ml_dtypes.bfloat16)

    par, v, r, s = np.meshgrid(np.arange(2), np.arange(27), np.arange(4), np.arange(4), indexing="ij")
    right = one_hot(4 * (2 * v + par) + r + s + 16, W_RIGHT)
    par, jj, r, s = np.meshgrid(np.arange(2), np.arange(18), np.arange(4), np.arange(4), indexing="ij")
    left = one_hot(4 * (2 * jj + par) + s + 24, ROWS)
    m, r, s = np.meshgrid(np.arange(10), np.arange(4), np.arange(4), indexing="ij")
    embed = one_hot(8 * m + r + 8, 96)
    jo, jj, r, s = np.meshgrid(np.arange(2), np.arange(16), np.arange(4), np.arange(4), indexing="ij")
    back = one_hot(r * 128 + 4 * (2 * jj + jo) + s, 512)
    return right, left, embed, back


def dot(a, b):
    return jnp.dot(a, b, preferred_element_type=F32)


def dot_nt(a, b):
    return lax.dot_general(a, b, NT, preferred_element_type=F32)


def kernel(
    feat, conv, outw, proj, emb, filt, head, target, mask, sel_r, sel_l, sel_e, sel_b,
    pred, loss,
    vhead, win, ewin, wconv, wout, wproj, wfilt, vtarget, vmask, vsel_r, vsel_l, vsel_e, vsel_b, vpred,
    rwin, first, gin, gpair, rr, ll, ee, pair, inner, red1, red2,
    local_sem, send_sem, recv_sem, pred_sem, s1, r1, s2, r2, vloss, loss_sem,
):
    d = lax.axis_index("diag")
    g = lax.axis_index("off")
    h = g // 2
    odd = g % 2
    core = odd
    z_lo = d // 16
    xy = d % 16
    x_at = xy // 4
    y_at = xy % 4
    z_at = 2 * h + z_lo

    feat_moves = [(0, -1, 96, 0), (1, 1, 0, 160)]
    embed_moves = [(2, -1, 48, 0), (3, 1, 0, 80)]
    even_moves = [(5, h, 0, 128, 32), (6, h + 1, 0, 96, 160), (4, h - 1, 96, 32, 0)]
    odd_moves = [(5, h + 1, 0, 128, 96), (4, h, 32, 96, 0), (6, h + 2, 0, 32, 224)]

    def on_diag(index):
        return jnp.logical_and(index >= 0, index < N_DIAG)

    def on_off(index):
        return jnp.logical_and(index >= 0, index < N_OFF)

    def remote(src, dst, number, peer):
        return pltpu.make_async_remote_copy(
            src_ref=src, dst_ref=dst, send_sem=send_sem.at[number], recv_sem=recv_sem.at[number],
            device_id=peer, device_id_type=pl.DeviceIdType.MESH,
        )

    def feat_move(number, ahead, start, to):
        return remote(win.at[pl.ds(32 + start, 32)], win.at[pl.ds(to, 32)], number, (d - ahead, g))

    def embed_move(number, ahead, start, to):
        return remote(ewin.at[pl.ds(16 + start, 16)], ewin.at[pl.ds(to, 16)], number, (d, g - ahead))

    def right_move(number, ahead, start, count, to):
        return remote(win.at[pl.ds(32 + start, count)], rwin.at[pl.ds(to, count)], number, (d - ahead, g))

    def each_right(act):
        pl.when(odd == 0)(lambda: [act(*one) for one in even_moves] and None)
        pl.when(odd == 1)(lambda: [act(*one) for one in odd_moves] and None)

    def wrapped(value, size):
        return jnp.where(value >= size, value - size, value)

    def far(step, size):
        return min(step, size - step)

    z_steps = sorted(((a, b) for a in range(8) for b in range(2) if a or b), key=lambda t: -far(t[0], 8) * 2 - t[1])
    xy_steps = sorted(((a, b) for a in range(4) for b in range(4) if a or b), key=lambda t: -far(t[0], 4) - far(t[1], 4))

    def z_peer(step):
        z = wrapped(z_at + step[0], 8)
        c = wrapped(core + step[1], 2)
        return (z % 2 * 16 + xy, z // 2 * 2 + c)

    def xy_peer(step):
        return (z_lo * 16 + wrapped(x_at + step[0], 4) * 4 + wrapped(y_at + step[1], 4), g)

    z_slot = z_at * 2 + core
    xy_slot = xy

    own = [
        pltpu.make_async_copy(feat, win.at[pl.ds(32, 128)], local_sem.at[16]),
        pltpu.make_async_copy(emb, ewin.at[pl.ds(16, 64)], local_sem.at[17]),
    ]
    for copy in own:
        copy.start()
    barrier = pltpu.get_barrier_semaphore()

    def greet(peer, times=1):
        pl.semaphore_signal(barrier, inc=times, device_id=peer, device_id_type=pl.DeviceIdType.MESH)

    def count_of(cond):
        return jnp.where(cond, 1, 0).astype(jnp.int32)

    for step in z_steps:
        greet(z_peer(step))
    total = jnp.int32(30)
    for reach in (-1, 1):
        ok = on_diag(d - reach)
        pl.when(ok)(lambda reach=reach: greet((d - reach, g)))
        total = total + count_of(ok)
        ok = on_off(g - reach)
        pl.when(ok)(lambda reach=reach: greet((d, g - reach)))
        total = total + count_of(ok)
    for step in range(3):
        ahead = h - 1 + odd + step
        ok_s = jnp.logical_and(on_diag(d - ahead), ahead != 0)
        ok_r = jnp.logical_and(on_diag(d + ahead), ahead != 0)
        pl.when(ok_s)(lambda ahead=ahead: greet((d - ahead, g)))
        pl.when(ok_r)(lambda ahead=ahead: greet((d + ahead, g)))
        total = total + count_of(ok_s) + count_of(ok_r)
    for step in xy_steps:
        greet(xy_peer(step))

    def right_begin(number, ahead, start, count, to):
        pl.when(jnp.logical_and(on_diag(d - ahead), ahead != 0))(
            lambda: right_move(number, ahead, start, count, to).start()
        )

    for copy in own:
        copy.wait()
    pl.semaphore_wait(barrier, total)
    for one in feat_moves:
        pl.when(on_diag(d - one[1]))(lambda one=one: feat_move(*one).start())
    each_right(right_begin)
    for one in embed_moves:
        pl.when(on_off(g - one[1]))(lambda one=one: embed_move(*one).start())

    loads = [(filt, wfilt), (head, vhead)]
    for layer in range(2):
        for tap in range(3):
            loads.append((conv.at[layer, tap], wconv.at[layer, :, pl.ds(128 * tap, 128)]))
    loads += [(outw, wout), (proj, wproj), (sel_l, vsel_l), (sel_e, vsel_e)]
    loads += [(sel_r, vsel_r), (sel_b, vsel_b), (target, vtarget), (mask, vmask)]
    copies = [pltpu.make_async_copy(a, b, local_sem.at[i]) for i, (a, b) in enumerate(loads)]
    for copy in copies:
        copy.start()

    copies[0].wait()
    copies[1].wait()
    lane = lax.broadcasted_iota(jnp.int32, (64, 128), 1)
    row64 = lax.broadcasted_iota(jnp.int32, (64, 128), 0)
    twice = jnp.where(lane % 64 == row64, 1.0, 0.0).astype(BF16)
    low = lane < 64
    taps = dot(wfilt[...], twice)

    def tap_of(layer, p, q):
        start = ((layer * 3 + p) * 3 + q) * 64
        return taps[start : start + 64]

    none = jnp.zeros((64, 128), F32)
    for jin in range(4):
        for jout in range(2):
            for kout in range(2):
                q = jin - jout
                base = (jout * 2 + kout) * 64
                rows = pl.ds(base, 64)
                if q < 0 or q > 2:
                    halves = (none, none)
                elif kout == 0:
                    halves = (jnp.where(low, tap_of(0, 0, q), tap_of(0, 1, q)), jnp.where(low, tap_of(0, 2, q), none))
                else:
                    halves = (jnp.where(low, none, tap_of(0, 0, q)), jnp.where(low, tap_of(0, 1, q), tap_of(0, 2, q)))
                first[rows, jin * 256 : jin * 256 + 128] = halves[0].astype(BF16)
                first[rows, jin * 256 + 128 : jin * 256 + 256] = halves[1].astype(BF16)

    head_row = vhead[0:1, :]
    h0 = head_row.astype(BF16).astype(F32)
    h1 = (head_row - h0).astype(BF16).astype(F32)
    h2 = (head_row - h0 - h1).astype(BF16).astype(F32)
    row8 = lax.broadcasted_iota(jnp.int32, (8, 64), 0)
    head8 = jnp.where(row8 == 0, h0, jnp.where(row8 == 1, h1, jnp.where(row8 == 2, h2, 0.0))).astype(BF16)
    head_twice = jnp.sum(dot(head8, twice), axis=0, keepdims=True)
    row96 = lax.broadcasted_iota(jnp.int32, (96, 128), 0)
    lane96 = lax.broadcasted_iota(jnp.int32, (96, 128), 1)
    k_out = row96 % 16
    kp = lane96 // 64
    q_of = row96 // 32

    def hi_lo(value):
        hi = value.astype(BF16).astype(F32)
        return hi, (value - hi).astype(BF16).astype(F32)

    folded = []
    for p in range(3):
        pieces = []
        for q in range(3):
            whole = jnp.sum(dot(head8, tap_of(1, p, q).astype(BF16)), axis=0, keepdims=True)
            for part in hi_lo(whole):
                pieces.append(jnp.broadcast_to(part, (16, 128)))
        folded.append(jnp.concatenate(pieces, axis=0))
    for m in range(9):
        p_of = 2 * m + kp - k_out
        block = jnp.zeros((96, 128), F32)
        for p in range(3):
            block = jnp.where(p_of == p, folded[p], block)
        gin[:, m * 128 : (m + 1) * 128] = block.astype(BF16)
    head_hi, head_lo = hi_lo(head_twice)
    head_block = jnp.where(row96 % 32 < 16, head_hi, head_lo)
    for m in range(8):
        block = jnp.where(jnp.logical_and(q_of == 1, 2 * m + kp == k_out), head_block, 0.0)
        gpair[:, m * 128 : (m + 1) * 128] = block.astype(BF16)

    for copy in copies[2:10]:
        copy.wait()
    for one in feat_moves:
        pl.when(on_diag(d + one[1]))(lambda one=one: feat_move(*one).wait_recv())

    def trunk(window, rows, start):
        at = lax.broadcasted_iota(jnp.int32, (rows, 1), 0) + start
        inside = jnp.logical_and(at >= 0, at < BINS)
        x = jnp.where(inside, window[...].astype(F32), 0.0)
        for layer, spread in ((0, 4), (1, 8)):
            y = dot(jnp.maximum(x, 0.0).astype(BF16), wconv[layer])
            c = pltpu.roll(y[:, 0:128], spread, 0) + y[:, 128:256] + pltpu.roll(y[:, 256:384], rows - spread, 0)
            v = jnp.maximum(c, 0.0).astype(BF16)
            x = jnp.where(inside, (x + dot(v, wout[layer])).astype(BF16).astype(F32), 0.0)
        value = dot(x.astype(BF16), wproj[...]).astype(BF16).astype(F32)
        return value, pltpu.roll(value, 64, 1)

    projected, swapped = trunk(win, ROWS, 128 * d - 32)

    for copy in copies[10:]:
        copy.wait()
    lane_l = lax.broadcasted_iota(jnp.int32, (ROWS, 128), 1) < 64
    left = jnp.where(lane_l, projected, swapped).astype(BF16)
    ll[...] = dot(vsel_l[...], left).reshape(2, 288, 128)
    for one in embed_moves:
        pl.when(on_off(g + one[1]))(lambda one=one: embed_move(*one).wait_recv())
    erow = lax.broadcasted_iota(jnp.int32, (96, 64), 0) + 64 * g - 16
    e_in = jnp.logical_and(erow >= 0, erow < BAND)
    e_val = jnp.where(e_in, ewin[...].astype(F32), 0.0).astype(BF16)
    e_two = dot(e_val, twice)
    e_two = jnp.where(lane96 < 64, e_two, pltpu.roll(e_two, 92, 0)).astype(BF16)
    ee[...] = dot(vsel_e[...], e_two).reshape(10, 16, 128)

    def right_finish(number, ahead, start, count, to):
        pl.when(jnp.logical_and(on_diag(d + ahead), ahead != 0))(
            lambda: right_move(number, ahead, start, count, to).wait_recv()
        )

    each_right(right_finish)

    def right_own(number, ahead, start, count, to):
        @pl.when(ahead == 0)
        def _():
            rwin[to : to + count, :] = win[32 + start : 32 + start + count, :]

    each_right(right_own)
    projected, swapped = trunk(rwin, W_RIGHT, 128 * d + 64 * g - 32)
    lane_r = lax.broadcasted_iota(jnp.int32, (W_RIGHT, 128), 1) < 64
    right = jnp.where(lane_r, swapped, pltpu.roll(projected, W_RIGHT - 4, 0)).astype(BF16)
    rr[...] = dot(vsel_r[...], right).reshape(2, 432, 128)

    for m in range(10):
        e = jnp.broadcast_to(ee[m][None], (18, 16, 128)).reshape(288, 128)
        for par in range(2):
            value = rr[par, m * 16 : m * 16 + 288, :] + ll[par] + e
            pair[par, :, m * 128 : (m + 1) * 128] = jnp.maximum(value, 0.0).astype(BF16)

    @pl.when(d == 0)
    def _():
        pair[:, 0:16, :] = jnp.zeros((2, 16, 1280), BF16)

    @pl.when(d == N_DIAG - 1)
    def _():
        pair[:, 272:288, :] = jnp.zeros((2, 16, 1280), BF16)

    @pl.when(g == 0)
    def _():
        pair[:, :, 0:128] = jnp.zeros((2, 288, 128), BF16)

    @pl.when(g == N_OFF - 1)
    def _():
        pair[:, :, 1152:1280] = jnp.zeros((2, 288, 128), BF16)

    for m in range(9):
        cols = slice(m * 128, m * 128 + 256)
        near = jnp.concatenate(
            [pair[0, 0:272, cols], pair[1, 0:272, cols], pair[0, 16:288, cols], pair[1, 16:288, cols]], axis=1
        )
        acc = jnp.maximum(dot_nt(near, first[...]), 0.0).astype(BF16)
        inner[0, :, m * 128 : (m + 1) * 128] = acc[:, 0:128]
        inner[1, :, m * 128 : (m + 1) * 128] = acc[:, 128:256]

    @pl.when(d == 0)
    def _():
        inner[0, 0:16, :] = jnp.zeros((16, 1152), BF16)

    @pl.when(d == N_DIAG - 1)
    def _():
        inner[1, 256:272, :] = jnp.zeros((16, 1152), BF16)

    lane272 = lax.broadcasted_iota(jnp.int32, (272, 128), 1)

    @pl.when(g == 0)
    def _():
        for par in range(2):
            inner[par, :, 0:128] = jnp.where(lane272 < 64, 0.0, inner[par, :, 0:128].astype(F32)).astype(BF16)

    @pl.when(g == N_OFF - 1)
    def _():
        for par in range(2):
            edge = inner[par, :, 1024:1152].astype(F32)
            inner[par, :, 1024:1152] = jnp.where(lane272 < 64, edge, 0.0).astype(BF16)

    def turned(value):
        full = jnp.concatenate([value, jnp.zeros((256, 32), F32)], axis=1)
        return jnp.transpose(full)

    sums = []
    for par in range(2):
        t = dot_nt(inner[par], gin[...])
        t = t + dot_nt(pair[1 - par, 16 * par : 16 * par + 272, 128:1152], gpair[...])
        sums.append((turned(t[0:256]), turned(t[16:272])))

    def both(value, q):
        return value[32 * q : 32 * q + 16] + value[32 * q + 16 : 32 * q + 32]

    (a0, a1), (b0, b1) = sums
    even = both(a0, 0) + both(b0, 1) + both(a1, 2)
    odds = both(b0, 0) + both(a1, 1) + both(b1, 2)
    flat = jnp.concatenate([even, odds], axis=1)
    p0 = flat.astype(BF16).astype(F32)
    p1 = (flat - p0).astype(BF16).astype(F32)
    p2 = flat - p0 - p1
    stacked = jnp.concatenate([p0, p1, p2], axis=0).astype(BF16)
    placed = dot(stacked, vsel_b[...])
    placed = placed[0:16] + placed[16:32] + placed[32:48]
    for r in range(4):
        vpred[pl.ds(r, 16, stride=4), :] = placed[:, r * 128 : (r + 1) * 128]
    out_copy = pltpu.make_async_copy(vpred, pred, pred_sem)
    out_copy.start()

    o_of = lax.broadcasted_iota(jnp.int32, (64, 128), 0) + 64 * g
    i_of = lax.broadcasted_iota(jnp.int32, (64, 128), 1) + 128 * d
    valid = jnp.where(o_of + i_of < BINS, vmask[...].astype(F32), 0.0)
    err = valid * (vpred[...] - vtarget[...]) ** 2

    def reduce_over(buf, slot, value, steps, peer, send, recv):
        buf[slot] = value
        for step in steps:
            pltpu.make_async_remote_copy(
                src_ref=buf.at[slot], dst_ref=buf.at[slot], send_sem=send, recv_sem=recv,
                device_id=peer(step), device_id_type=pl.DeviceIdType.MESH,
            ).start()
        pltpu.make_async_copy(buf.at[pl.ds(0, 15)], buf.at[pl.ds(0, 15)], recv).wait()
        return jnp.sum(buf[...], axis=0)

    def reduce_retire(buf, send):
        pltpu.make_async_copy(buf.at[pl.ds(0, 15)], buf.at[pl.ds(0, 15)], send).wait()

    partial = jnp.sum(err.reshape(8, 8, 128), axis=0)
    partial = reduce_over(red1, z_slot, partial, z_steps, z_peer, s1, r1)
    partial = reduce_over(red2, xy_slot, partial, xy_steps, xy_peer, s2, r2)
    vloss[...] = partial
    loss_copy = pltpu.make_async_copy(vloss, loss, loss_sem)
    loss_copy.start()

    out_copy.wait()
    loss_copy.wait()
    for one in feat_moves:
        pl.when(on_diag(d - one[1]))(lambda one=one: feat_move(*one).wait_send())
    for one in embed_moves:
        pl.when(on_off(g - one[1]))(lambda one=one: embed_move(*one).wait_send())

    def right_retire(number, ahead, start, count, to):
        pl.when(jnp.logical_and(on_diag(d - ahead), ahead != 0))(
            lambda: right_move(number, ahead, start, count, to).wait_send()
        )

    each_right(right_retire)
    reduce_retire(red1, s1)
    reduce_retire(red2, s2)


def finish(pred_in, parts, pred, loss):
    pred[...] = pred_in[...]
    loss[0, 0] = jnp.sum(parts[...]) / (BAND * BINS)


def body(features, conv_weight, out_weight, proj_weight, offset_embed, pair_filter_weight, head_weight, target, cell_mask):
    vmem = pl.BlockSpec(memory_space=pltpu.VMEM)
    anywhere = pl.BlockSpec(memory_space=pltpu.HBM)
    picks = [jnp.asarray(value) for value in selections()]
    pred, loss = pl.pallas_call(
        kernel,
        out_shape=(jax.ShapeDtypeStruct((64, 128), F32), jax.ShapeDtypeStruct((8, 128), F32)),
        in_specs=[anywhere] * 13,
        out_specs=(anywhere, anywhere),
        scratch_shapes=[
            pltpu.VMEM((1, CP), F32),
            pltpu.VMEM((ROWS, D), BF16),
            pltpu.VMEM((96, CP), BF16),
            pltpu.VMEM((2, D, 384), BF16),
            pltpu.VMEM((2, 128, D), BF16),
            pltpu.VMEM((D, 128), BF16),
            pltpu.VMEM((1152, CP), BF16),
            pltpu.VMEM((64, 128), F32),
            pltpu.VMEM((64, 128), jnp.int32),
            pltpu.VMEM((864, W_RIGHT), BF16),
            pltpu.VMEM((576, ROWS), BF16),
            pltpu.VMEM((160, 96), BF16),
            pltpu.VMEM((512, 512), BF16),
            pltpu.VMEM((64, 128), F32),
            pltpu.VMEM((W_RIGHT, D), BF16),
            pltpu.VMEM((256, 1024), BF16),
            pltpu.VMEM((96, 1152), BF16),
            pltpu.VMEM((96, 1024), BF16),
            pltpu.VMEM((2, 432, 128), F32),
            pltpu.VMEM((2, 288, 128), F32),
            pltpu.VMEM((10, 16, 128), F32),
            pltpu.VMEM((2, 288, 1280), BF16),
            pltpu.VMEM((2, 272, 1152), BF16),
            pltpu.VMEM((16, 8, 128), F32),
            pltpu.VMEM((16, 8, 128), F32),
            pltpu.SemaphoreType.DMA((18,)),
            pltpu.SemaphoreType.DMA((7,)),
            pltpu.SemaphoreType.DMA((7,)),
            pltpu.SemaphoreType.DMA,
            pltpu.SemaphoreType.DMA,
            pltpu.SemaphoreType.DMA,
            pltpu.SemaphoreType.DMA,
            pltpu.SemaphoreType.DMA,
            pltpu.VMEM((8, 128), F32),
            pltpu.SemaphoreType.DMA,
        ],
        compiler_params=pltpu.CompilerParams(
            collective_id=0, has_side_effects=True, vmem_limit_bytes=64 * 1024 * 1024
        ),
        name="contact_block",
    )(
        features, conv_weight, out_weight, proj_weight, offset_embed,
        pair_filter_weight.reshape(1152, CP), head_weight.reshape(1, CP), target, cell_mask, *picks,
    )
    pred, loss = pl.pallas_call(
        finish,
        out_shape=(jax.ShapeDtypeStruct((64, 128), F32), jax.ShapeDtypeStruct((1, 1), F32)),
        in_specs=[vmem, vmem],
        out_specs=(vmem, pl.BlockSpec(memory_space=pltpu.SMEM)),
        compiler_params=pltpu.CompilerParams(vmem_limit_bytes=64 * 1024 * 1024),
        name="finish",
    )(pred, loss)
    return pred, loss[0, 0]


def solution(mesh):
    in_specs = (P("diag", None), P(), P(), P(), P("off", None), P(), P(), P("off", "diag"), P("off", "diag"))
    out_specs = (P("off", "diag"), P())
    return jax.shard_map(body, mesh=mesh, in_specs=in_specs, out_specs=out_specs, check_vma=False)
```

```python
import jax
import jax.numpy as jnp
import ml_dtypes
import numpy as np
from jax import lax
from jax.experimental import pallas as pl
from jax.experimental.pallas import tpu as pltpu
from jax.sharding import PartitionSpec as P

BINS = 4096
BAND = 512
CP = 64
D = 256
N_DIAG = 32
N_OFF = 8
ROWS = 192
W_RIGHT = 256
F32 = jnp.float32
BF16 = jnp.bfloat16
NT = (((1,), (1,)), ((), ()))


def selections():
    def one_hot(index, width):
        index = np.asarray(index).reshape(-1)
        return (index[:, None] == np.arange(width)[None, :]).astype(ml_dtypes.bfloat16)

    par, v, r, s = np.meshgrid(np.arange(2), np.arange(27), np.arange(4), np.arange(4), indexing="ij")
    right = one_hot(4 * (2 * v + par) + r + s + 16, W_RIGHT)
    par, jj, r, s = np.meshgrid(np.arange(2), np.arange(18), np.arange(4), np.arange(4), indexing="ij")
    left = one_hot(4 * (2 * jj + par) + s + 24, ROWS)
    m, r, s = np.meshgrid(np.arange(10), np.arange(4), np.arange(4), indexing="ij")
    embed = one_hot(8 * m + r + 8, 96)
    jo, jj, r, s = np.meshgrid(np.arange(2), np.arange(16), np.arange(4), np.arange(4), indexing="ij")
    back = one_hot(r * 128 + 4 * (2 * jj + jo) + s, 512)
    return right, left, embed, back


def dot(a, b):
    return jnp.dot(a, b, preferred_element_type=F32)


def dot_nt(a, b):
    return lax.dot_general(a, b, NT, preferred_element_type=F32)


def kernel(
    feat, conv, outw, proj, emb, filt, head, target, mask, sel_r, sel_l, sel_e, sel_b,
    pred, loss,
    vhead, win, ewin, wconv, wout, wproj, wfilt, vtarget, vmask, vsel_r, vsel_l, vsel_e, vsel_b, vpred,
    rwin, first, gin, gpair, rr, ll, ee, pair, inner, red1,
    local_sem, send_sem, recv_sem, pred_sem, s1, r1, s2, r2, vloss, loss_sem,
):
    d = lax.axis_index("diag")
    g = lax.axis_index("off")
    h = g // 2
    odd = g % 2
    core = odd
    z_lo = d // 16
    xy = d % 16
    x_at = xy // 4
    y_at = xy % 4
    z_at = 2 * h + z_lo

    feat_moves = [(0, -1, 96, 0), (1, 1, 0, 160)]
    embed_moves = [(2, -1, 48, 0), (3, 1, 0, 80)]
    even_moves = [(5, h, 0, 128, 32), (6, h + 1, 0, 96, 160), (4, h - 1, 96, 32, 0)]
    odd_moves = [(5, h + 1, 0, 128, 96), (4, h, 32, 96, 0), (6, h + 2, 0, 32, 224)]

    def on_diag(index):
        return jnp.logical_and(index >= 0, index < N_DIAG)

    def on_off(index):
        return jnp.logical_and(index >= 0, index < N_OFF)

    def remote(src, dst, number, peer):
        return pltpu.make_async_remote_copy(
            src_ref=src, dst_ref=dst, send_sem=send_sem.at[number], recv_sem=recv_sem.at[number],
            device_id=peer, device_id_type=pl.DeviceIdType.MESH,
        )

    def feat_move(number, ahead, start, to):
        return remote(win.at[pl.ds(32 + start, 32)], win.at[pl.ds(to, 32)], number, (d - ahead, g))

    def embed_move(number, ahead, start, to):
        return remote(ewin.at[pl.ds(16 + start, 16)], ewin.at[pl.ds(to, 16)], number, (d, g - ahead))

    def right_move(number, ahead, start, count, to):
        return remote(win.at[pl.ds(32 + start, count)], rwin.at[pl.ds(to, count)], number, (d - ahead, g))

    def each_right(act):
        pl.when(odd == 0)(lambda: [act(*one) for one in even_moves] and None)
        pl.when(odd == 1)(lambda: [act(*one) for one in odd_moves] and None)

    def wrapped(value, size):
        return jnp.where(value >= size, value - size, value)

    def far(step, size):
        return min(step, size - step)

    z_steps = sorted(((a, b) for a in range(8) for b in range(2) if a or b), key=lambda t: -far(t[0], 8) * 2 - t[1])
    xy_steps = sorted(((a, b) for a in range(4) for b in range(4) if a or b), key=lambda t: -far(t[0], 4) - far(t[1], 4))

    def z_peer(step):
        z = wrapped(z_at + step[0], 8)
        c = wrapped(core + step[1], 2)
        return (z % 2 * 16 + xy, z // 2 * 2 + c)

    def xy_peer(step):
        return (z_lo * 16 + wrapped(x_at + step[0], 4) * 4 + wrapped(y_at + step[1], 4), g)

    z_slot = z_at * 2 + core
    xy_slot = xy

    own = [
        pltpu.make_async_copy(feat, win.at[pl.ds(32, 128)], local_sem.at[16]),
        pltpu.make_async_copy(emb, ewin.at[pl.ds(16, 64)], local_sem.at[17]),
    ]
    for copy in own:
        copy.start()
    barrier = pltpu.get_barrier_semaphore()

    def greet(peer, times=1):
        pl.semaphore_signal(barrier, inc=times, device_id=peer, device_id_type=pl.DeviceIdType.MESH)

    def count_of(cond):
        return jnp.where(cond, 1, 0).astype(jnp.int32)

    for step in z_steps:
        greet(z_peer(step))
    total = jnp.int32(30)
    for reach in (-1, 1):
        ok = on_diag(d - reach)
        pl.when(ok)(lambda reach=reach: greet((d - reach, g)))
        total = total + count_of(ok)
        ok = on_off(g - reach)
        pl.when(ok)(lambda reach=reach: greet((d, g - reach)))
        total = total + count_of(ok)
    for step in range(3):
        ahead = h - 1 + odd + step
        ok_s = jnp.logical_and(on_diag(d - ahead), ahead != 0)
        ok_r = jnp.logical_and(on_diag(d + ahead), ahead != 0)
        pl.when(ok_s)(lambda ahead=ahead: greet((d - ahead, g)))
        pl.when(ok_r)(lambda ahead=ahead: greet((d + ahead, g)))
        total = total + count_of(ok_s) + count_of(ok_r)
    for step in xy_steps:
        greet(xy_peer(step))

    def right_begin(number, ahead, start, count, to):
        pl.when(jnp.logical_and(on_diag(d - ahead), ahead != 0))(
            lambda: right_move(number, ahead, start, count, to).start()
        )

    for copy in own:
        copy.wait()
    pl.semaphore_wait(barrier, total)
    for one in feat_moves:
        pl.when(on_diag(d - one[1]))(lambda one=one: feat_move(*one).start())
    each_right(right_begin)
    for one in embed_moves:
        pl.when(on_off(g - one[1]))(lambda one=one: embed_move(*one).start())

    loads = [(filt, wfilt), (head, vhead)]
    for layer in range(2):
        for tap in range(3):
            loads.append((conv.at[layer, tap], wconv.at[layer, :, pl.ds(128 * tap, 128)]))
    loads += [(outw, wout), (proj, wproj), (sel_l, vsel_l), (sel_e, vsel_e)]
    loads += [(sel_r, vsel_r), (sel_b, vsel_b), (target, vtarget), (mask, vmask)]
    copies = [pltpu.make_async_copy(a, b, local_sem.at[i]) for i, (a, b) in enumerate(loads)]
    for copy in copies:
        copy.start()

    copies[0].wait()
    copies[1].wait()
    lane = lax.broadcasted_iota(jnp.int32, (64, 128), 1)
    row64 = lax.broadcasted_iota(jnp.int32, (64, 128), 0)
    twice = jnp.where(lane % 64 == row64, 1.0, 0.0).astype(BF16)
    low = lane < 64
    taps = dot(wfilt[...], twice)

    def tap_of(layer, p, q):
        start = ((layer * 3 + p) * 3 + q) * 64
        return taps[start : start + 64]

    none = jnp.zeros((64, 128), F32)
    for jin in range(4):
        for jout in range(2):
            for kout in range(2):
                q = jin - jout
                base = (jout * 2 + kout) * 64
                rows = pl.ds(base, 64)
                if q < 0 or q > 2:
                    halves = (none, none)
                elif kout == 0:
                    halves = (jnp.where(low, tap_of(0, 0, q), tap_of(0, 1, q)), jnp.where(low, tap_of(0, 2, q), none))
                else:
                    halves = (jnp.where(low, none, tap_of(0, 0, q)), jnp.where(low, tap_of(0, 1, q), tap_of(0, 2, q)))
                first[rows, jin * 256 : jin * 256 + 128] = halves[0].astype(BF16)
                first[rows, jin * 256 + 128 : jin * 256 + 256] = halves[1].astype(BF16)

    head_row = vhead[0:1, :]
    h0 = head_row.astype(BF16).astype(F32)
    h1 = (head_row - h0).astype(BF16).astype(F32)
    h2 = (head_row - h0 - h1).astype(BF16).astype(F32)
    row8 = lax.broadcasted_iota(jnp.int32, (8, 64), 0)
    head8 = jnp.where(row8 == 0, h0, jnp.where(row8 == 1, h1, jnp.where(row8 == 2, h2, 0.0))).astype(BF16)
    head_twice = jnp.sum(dot(head8, twice), axis=0, keepdims=True)
    row96 = lax.broadcasted_iota(jnp.int32, (96, 128), 0)
    lane96 = lax.broadcasted_iota(jnp.int32, (96, 128), 1)
    k_out = row96 % 16
    kp = lane96 // 64
    q_of = row96 // 32

    def hi_lo(value):
        hi = value.astype(BF16).astype(F32)
        return hi, (value - hi).astype(BF16).astype(F32)

    folded = []
    for p in range(3):
        pieces = []
        for q in range(3):
            whole = jnp.sum(dot(head8, tap_of(1, p, q).astype(BF16)), axis=0, keepdims=True)
            for part in hi_lo(whole):
                pieces.append(jnp.broadcast_to(part, (16, 128)))
        folded.append(jnp.concatenate(pieces, axis=0))
    for m in range(9):
        p_of = 2 * m + kp - k_out
        block = jnp.zeros((96, 128), F32)
        for p in range(3):
            block = jnp.where(p_of == p, folded[p], block)
        gin[:, m * 128 : (m + 1) * 128] = block.astype(BF16)
    head_hi, head_lo = hi_lo(head_twice)
    head_block = jnp.where(row96 % 32 < 16, head_hi, head_lo)
    for m in range(8):
        block = jnp.where(jnp.logical_and(q_of == 1, 2 * m + kp == k_out), head_block, 0.0)
        gpair[:, m * 128 : (m + 1) * 128] = block.astype(BF16)

    for copy in copies[2:10]:
        copy.wait()
    for one in feat_moves:
        pl.when(on_diag(d + one[1]))(lambda one=one: feat_move(*one).wait_recv())

    def trunk(window, rows, start):
        at = lax.broadcasted_iota(jnp.int32, (rows, 1), 0) + start
        inside = jnp.logical_and(at >= 0, at < BINS)
        x = jnp.where(inside, window[...].astype(F32), 0.0)
        for layer, spread in ((0, 4), (1, 8)):
            y = dot(jnp.maximum(x, 0.0).astype(BF16), wconv[layer])
            c = pltpu.roll(y[:, 0:128], spread, 0) + y[:, 128:256] + pltpu.roll(y[:, 256:384], rows - spread, 0)
            v = jnp.maximum(c, 0.0).astype(BF16)
            x = jnp.where(inside, (x + dot(v, wout[layer])).astype(BF16).astype(F32), 0.0)
        value = dot(x.astype(BF16), wproj[...]).astype(BF16).astype(F32)
        return value, pltpu.roll(value, 64, 1)

    projected, swapped = trunk(win, ROWS, 128 * d - 32)

    for copy in copies[10:]:
        copy.wait()
    lane_l = lax.broadcasted_iota(jnp.int32, (ROWS, 128), 1) < 64
    left = jnp.where(lane_l, projected, swapped).astype(BF16)
    ll[...] = dot(vsel_l[...], left).reshape(2, 288, 128)
    for one in embed_moves:
        pl.when(on_off(g + one[1]))(lambda one=one: embed_move(*one).wait_recv())
    erow = lax.broadcasted_iota(jnp.int32, (96, 64), 0) + 64 * g - 16
    e_in = jnp.logical_and(erow >= 0, erow < BAND)
    e_val = jnp.where(e_in, ewin[...].astype(F32), 0.0).astype(BF16)
    e_two = dot(e_val, twice)
    e_two = jnp.where(lane96 < 64, e_two, pltpu.roll(e_two, 92, 0)).astype(BF16)
    ee[...] = dot(vsel_e[...], e_two).reshape(10, 16, 128)

    def right_finish(number, ahead, start, count, to):
        pl.when(jnp.logical_and(on_diag(d + ahead), ahead != 0))(
            lambda: right_move(number, ahead, start, count, to).wait_recv()
        )

    each_right(right_finish)

    def right_own(number, ahead, start, count, to):
        @pl.when(ahead == 0)
        def _():
            rwin[to : to + count, :] = win[32 + start : 32 + start + count, :]

    each_right(right_own)
    projected, swapped = trunk(rwin, W_RIGHT, 128 * d + 64 * g - 32)
    lane_r = lax.broadcasted_iota(jnp.int32, (W_RIGHT, 128), 1) < 64
    right = jnp.where(lane_r, swapped, pltpu.roll(projected, W_RIGHT - 4, 0)).astype(BF16)
    rr[...] = dot(vsel_r[...], right).reshape(2, 432, 128)

    for m in range(10):
        e = jnp.broadcast_to(ee[m][None], (18, 16, 128)).reshape(288, 128)
        for par in range(2):
            value = rr[par, m * 16 : m * 16 + 288, :] + ll[par] + e
            pair[par, :, m * 128 : (m + 1) * 128] = jnp.maximum(value, 0.0).astype(BF16)

    @pl.when(d == 0)
    def _():
        pair[:, 0:16, :] = jnp.zeros((2, 16, 1280), BF16)

    @pl.when(d == N_DIAG - 1)
    def _():
        pair[:, 272:288, :] = jnp.zeros((2, 16, 1280), BF16)

    @pl.when(g == 0)
    def _():
        pair[:, :, 0:128] = jnp.zeros((2, 288, 128), BF16)

    @pl.when(g == N_OFF - 1)
    def _():
        pair[:, :, 1152:1280] = jnp.zeros((2, 288, 128), BF16)

    for m in range(9):
        cols = slice(m * 128, m * 128 + 256)
        near = jnp.concatenate(
            [pair[0, 0:272, cols], pair[1, 0:272, cols], pair[0, 16:288, cols], pair[1, 16:288, cols]], axis=1
        )
        acc = jnp.maximum(dot_nt(near, first[...]), 0.0).astype(BF16)
        inner[0, :, m * 128 : (m + 1) * 128] = acc[:, 0:128]
        inner[1, :, m * 128 : (m + 1) * 128] = acc[:, 128:256]

    @pl.when(d == 0)
    def _():
        inner[0, 0:16, :] = jnp.zeros((16, 1152), BF16)

    @pl.when(d == N_DIAG - 1)
    def _():
        inner[1, 256:272, :] = jnp.zeros((16, 1152), BF16)

    lane272 = lax.broadcasted_iota(jnp.int32, (272, 128), 1)

    @pl.when(g == 0)
    def _():
        for par in range(2):
            inner[par, :, 0:128] = jnp.where(lane272 < 64, 0.0, inner[par, :, 0:128].astype(F32)).astype(BF16)

    @pl.when(g == N_OFF - 1)
    def _():
        for par in range(2):
            edge = inner[par, :, 1024:1152].astype(F32)
            inner[par, :, 1024:1152] = jnp.where(lane272 < 64, edge, 0.0).astype(BF16)

    def turned(value):
        full = jnp.concatenate([value, jnp.zeros((256, 32), F32)], axis=1)
        return jnp.transpose(full)

    sums = []
    for par in range(2):
        t = dot_nt(inner[par], gin[...])
        t = t + dot_nt(pair[1 - par, 16 * par : 16 * par + 272, 128:1152], gpair[...])
        sums.append((turned(t[0:256]), turned(t[16:272])))

    def both(value, q):
        return value[32 * q : 32 * q + 16] + value[32 * q + 16 : 32 * q + 32]

    (a0, a1), (b0, b1) = sums
    even = both(a0, 0) + both(b0, 1) + both(a1, 2)
    odds = both(b0, 0) + both(a1, 1) + both(b1, 2)
    flat = jnp.concatenate([even, odds], axis=1)
    p0 = flat.astype(BF16).astype(F32)
    p1 = (flat - p0).astype(BF16).astype(F32)
    p2 = flat - p0 - p1
    stacked = jnp.concatenate([p0, p1, p2], axis=0).astype(BF16)
    placed = dot(stacked, vsel_b[...])
    placed = placed[0:16] + placed[16:32] + placed[32:48]
    for r in range(4):
        vpred[pl.ds(r, 16, stride=4), :] = placed[:, r * 128 : (r + 1) * 128]
    out_copy = pltpu.make_async_copy(vpred, pred, pred_sem)
    out_copy.start()

    o_of = lax.broadcasted_iota(jnp.int32, (64, 128), 0) + 64 * g
    i_of = lax.broadcasted_iota(jnp.int32, (64, 128), 1) + 128 * d
    valid = jnp.where(o_of + i_of < BINS, vmask[...].astype(F32), 0.0)
    err = valid * (vpred[...] - vtarget[...]) ** 2

    def spread(source, buf, steps, slot, peer, send, recv):
        for step in steps:
            pltpu.make_async_remote_copy(
                src_ref=source, dst_ref=buf.at[slot], send_sem=send, recv_sem=recv,
                device_id=peer(step), device_id_type=pl.DeviceIdType.MESH,
            ).start()

    def settled(buf, sem):
        pltpu.make_async_copy(buf.at[pl.ds(0, 15)], buf.at[pl.ds(0, 15)], sem).wait()

    red1[z_slot] = jnp.sum(err, axis=0, keepdims=True)
    spread(red1.at[z_slot], red1, z_steps, z_slot, z_peer, s1, r1)
    settled(red1, r1)
    vloss[...] = jnp.sum(red1[...], axis=0)
    spread(vloss, loss, xy_steps, xy_slot, xy_peer, s2, r2)
    own_part = pltpu.make_async_copy(vloss, loss.at[xy_slot], loss_sem)
    own_part.start()

    out_copy.wait()
    for one in feat_moves:
        pl.when(on_diag(d - one[1]))(lambda one=one: feat_move(*one).wait_send())
    for one in embed_moves:
        pl.when(on_off(g - one[1]))(lambda one=one: embed_move(*one).wait_send())

    def right_retire(number, ahead, start, count, to):
        pl.when(jnp.logical_and(on_diag(d - ahead), ahead != 0))(
            lambda: right_move(number, ahead, start, count, to).wait_send()
        )

    each_right(right_retire)
    settled(red1, s1)
    settled(loss, s2)
    own_part.wait()
    settled(loss, r2)


def finish(pred_in, parts, pred, loss):
    pred[...] = pred_in[...]
    loss[0, 0] = jnp.sum(parts[...]) / (BAND * BINS)


def body(features, conv_weight, out_weight, proj_weight, offset_embed, pair_filter_weight, head_weight, target, cell_mask):
    vmem = pl.BlockSpec(memory_space=pltpu.VMEM)
    anywhere = pl.BlockSpec(memory_space=pltpu.HBM)
    picks = [jnp.asarray(value) for value in selections()]
    pred, loss = pl.pallas_call(
        kernel,
        out_shape=(jax.ShapeDtypeStruct((64, 128), F32), jax.ShapeDtypeStruct((16, 1, 128), F32)),
        in_specs=[anywhere] * 13,
        out_specs=(anywhere, anywhere),
        scratch_shapes=[
            pltpu.VMEM((1, CP), F32),
            pltpu.VMEM((ROWS, D), BF16),
            pltpu.VMEM((96, CP), BF16),
            pltpu.VMEM((2, D, 384), BF16),
            pltpu.VMEM((2, 128, D), BF16),
            pltpu.VMEM((D, 128), BF16),
            pltpu.VMEM((1152, CP), BF16),
            pltpu.VMEM((64, 128), F32),
            pltpu.VMEM((64, 128), jnp.int32),
            pltpu.VMEM((864, W_RIGHT), BF16),
            pltpu.VMEM((576, ROWS), BF16),
            pltpu.VMEM((160, 96), BF16),
            pltpu.VMEM((512, 512), BF16),
            pltpu.VMEM((64, 128), F32),
            pltpu.VMEM((W_RIGHT, D), BF16),
            pltpu.VMEM((256, 1024), BF16),
            pltpu.VMEM((96, 1152), BF16),
            pltpu.VMEM((96, 1024), BF16),
            pltpu.VMEM((2, 432, 128), F32),
            pltpu.VMEM((2, 288, 128), F32),
            pltpu.VMEM((10, 16, 128), F32),
            pltpu.VMEM((2, 288, 1280), BF16),
            pltpu.VMEM((2, 272, 1152), BF16),
            pltpu.VMEM((16, 1, 128), F32),
            pltpu.SemaphoreType.DMA((18,)),
            pltpu.SemaphoreType.DMA((7,)),
            pltpu.SemaphoreType.DMA((7,)),
            pltpu.SemaphoreType.DMA,
            pltpu.SemaphoreType.DMA,
            pltpu.SemaphoreType.DMA,
            pltpu.SemaphoreType.DMA,
            pltpu.SemaphoreType.DMA,
            pltpu.VMEM((1, 128), F32),
            pltpu.SemaphoreType.DMA,
        ],
        compiler_params=pltpu.CompilerParams(
            collective_id=0, has_side_effects=True, vmem_limit_bytes=64 * 1024 * 1024
        ),
        name="contact_block",
    )(
        features, conv_weight, out_weight, proj_weight, offset_embed,
        pair_filter_weight.reshape(1152, CP), head_weight.reshape(1, CP), target, cell_mask, *picks,
    )
    pred, loss = pl.pallas_call(
        finish,
        out_shape=(jax.ShapeDtypeStruct((64, 128), F32), jax.ShapeDtypeStruct((1, 1), F32)),
        in_specs=[vmem, vmem],
        out_specs=(vmem, pl.BlockSpec(memory_space=pltpu.SMEM)),
        compiler_params=pltpu.CompilerParams(vmem_limit_bytes=64 * 1024 * 1024),
        name="finish",
    )(pred, loss)
    return pred, loss[0, 0]


def solution(mesh):
    in_specs = (P("diag", None), P(), P(), P(), P("off", None), P(), P(), P("off", "diag"), P("off", "diag"))
    out_specs = (P("off", "diag"), P())
    return jax.shard_map(body, mesh=mesh, in_specs=in_specs, out_specs=out_specs, check_vma=False)
```

```python
import jax
import jax.numpy as jnp
import ml_dtypes
import numpy as np
from jax import lax
from jax.experimental import pallas as pl
from jax.experimental.pallas import tpu as pltpu
from jax.sharding import PartitionSpec as P

BINS = 4096
BAND = 512
CP = 64
D = 256
N_DIAG = 32
N_OFF = 8
ROWS = 192
W_RIGHT = 256
F32 = jnp.float32
BF16 = jnp.bfloat16
NT = (((1,), (1,)), ((), ()))


def selections():
    def one_hot(index, width):
        index = np.asarray(index).reshape(-1)
        return (index[:, None] == np.arange(width)[None, :]).astype(ml_dtypes.bfloat16)

    par, v, r, s = np.meshgrid(np.arange(2), np.arange(27), np.arange(4), np.arange(4), indexing="ij")
    right = one_hot(4 * (2 * v + par) + r + s + 16, W_RIGHT)
    par, jj, r, s = np.meshgrid(np.arange(2), np.arange(18), np.arange(4), np.arange(4), indexing="ij")
    left = one_hot(4 * (2 * jj + par) + s + 24, ROWS)
    m, r, s = np.meshgrid(np.arange(10), np.arange(4), np.arange(4), indexing="ij")
    embed = one_hot(8 * m + r + 8, 96)
    jo, jj, r, s = np.meshgrid(np.arange(2), np.arange(16), np.arange(4), np.arange(4), indexing="ij")
    back = one_hot(r * 128 + 4 * (2 * jj + jo) + s, 512)
    return right, left, embed, back


def dot(a, b):
    return jnp.dot(a, b, preferred_element_type=F32)


def dot_nt(a, b):
    return lax.dot_general(a, b, NT, preferred_element_type=F32)


def kernel(
    feat, conv, outw, proj, emb, filt, head, target, mask, sel_r, sel_l, sel_e, sel_b,
    pred, loss,
    vhead, win, ewin, wconv, wout, wproj, wfilt, vtarget, vmask, vsel_r, vsel_l, vsel_e, vsel_b, vpred,
    rwin, first, gin, gpair, rr, ll, ee, pair, inner, red1,
    local_sem, send_sem, recv_sem, pred_sem, s1, r1, s2, r2, vloss, loss_sem,
):
    d = lax.axis_index("diag")
    g = lax.axis_index("off")
    h = g // 2
    odd = g % 2
    core = odd
    z_lo = d // 16
    xy = d % 16
    x_at = xy // 4
    y_at = xy % 4
    z_at = 2 * h + z_lo

    feat_moves = [(0, -1, 96, 0), (1, 1, 0, 160)]
    embed_moves = [(2, -1, 48, 0), (3, 1, 0, 80)]
    even_moves = [(5, h, 0, 128, 32), (6, h + 1, 0, 96, 160), (4, h - 1, 96, 32, 0)]
    odd_moves = [(5, h + 1, 0, 128, 96), (4, h, 32, 96, 0), (6, h + 2, 0, 32, 224)]

    def on_diag(index):
        return jnp.logical_and(index >= 0, index < N_DIAG)

    def on_off(index):
        return jnp.logical_and(index >= 0, index < N_OFF)

    def remote(src, dst, number, peer):
        return pltpu.make_async_remote_copy(
            src_ref=src, dst_ref=dst, send_sem=send_sem.at[number], recv_sem=recv_sem.at[number],
            device_id=peer, device_id_type=pl.DeviceIdType.MESH,
        )

    def feat_move(number, ahead, start, to):
        return remote(win.at[pl.ds(32 + start, 32)], win.at[pl.ds(to, 32)], number, (d - ahead, g))

    def embed_move(number, ahead, start, to):
        return remote(ewin.at[pl.ds(16 + start, 16)], ewin.at[pl.ds(to, 16)], number, (d, g - ahead))

    def right_move(number, ahead, start, count, to):
        return remote(win.at[pl.ds(32 + start, count)], rwin.at[pl.ds(to, count)], number, (d - ahead, g))

    def each_right(act):
        pl.when(odd == 0)(lambda: [act(*one) for one in even_moves] and None)
        pl.when(odd == 1)(lambda: [act(*one) for one in odd_moves] and None)

    def wrapped(value, size):
        return jnp.where(value >= size, value - size, value)

    def far(step, size):
        return min(step, size - step)

    z_steps = sorted(((a, b) for a in range(8) for b in range(2) if a or b), key=lambda t: -far(t[0], 8) * 2 - t[1])
    xy_steps = sorted(((a, b) for a in range(4) for b in range(4) if a or b), key=lambda t: -far(t[0], 4) - far(t[1], 4))

    def z_peer(step):
        z = wrapped(z_at + step[0], 8)
        c = wrapped(core + step[1], 2)
        return (z % 2 * 16 + xy, z // 2 * 2 + c)

    def xy_peer(step):
        return (z_lo * 16 + wrapped(x_at + step[0], 4) * 4 + wrapped(y_at + step[1], 4), g)

    z_slot = z_at * 2 + core
    xy_slot = xy

    own = [
        pltpu.make_async_copy(feat, win.at[pl.ds(32, 128)], local_sem.at[16]),
        pltpu.make_async_copy(emb, ewin.at[pl.ds(16, 64)], local_sem.at[17]),
    ]
    for copy in own:
        copy.start()
    barrier = pltpu.get_barrier_semaphore()

    def greet(peer, times=1):
        pl.semaphore_signal(barrier, inc=times, device_id=peer, device_id_type=pl.DeviceIdType.MESH)

    def count_of(cond):
        return jnp.where(cond, 1, 0).astype(jnp.int32)

    for step in z_steps:
        greet(z_peer(step))
    total = jnp.int32(30)
    for reach in (-1, 1):
        ok = on_diag(d - reach)
        pl.when(ok)(lambda reach=reach: greet((d - reach, g)))
        total = total + count_of(ok)
        ok = on_off(g - reach)
        pl.when(ok)(lambda reach=reach: greet((d, g - reach)))
        total = total + count_of(ok)
    for step in range(3):
        ahead = h - 1 + odd + step
        ok_s = jnp.logical_and(on_diag(d - ahead), ahead != 0)
        ok_r = jnp.logical_and(on_diag(d + ahead), ahead != 0)
        pl.when(ok_s)(lambda ahead=ahead: greet((d - ahead, g)))
        pl.when(ok_r)(lambda ahead=ahead: greet((d + ahead, g)))
        total = total + count_of(ok_s) + count_of(ok_r)
    for step in xy_steps:
        greet(xy_peer(step))

    def right_begin(number, ahead, start, count, to):
        pl.when(jnp.logical_and(on_diag(d - ahead), ahead != 0))(
            lambda: right_move(number, ahead, start, count, to).start()
        )

    for copy in own:
        copy.wait()
    pl.semaphore_wait(barrier, total)
    for one in feat_moves:
        pl.when(on_diag(d - one[1]))(lambda one=one: feat_move(*one).start())
    each_right(right_begin)
    for one in embed_moves:
        pl.when(on_off(g - one[1]))(lambda one=one: embed_move(*one).start())

    loads = [(filt, wfilt), (head, vhead)]
    for layer in range(2):
        for tap in range(3):
            loads.append((conv.at[layer, tap], wconv.at[layer, :, pl.ds(128 * tap, 128)]))
    loads += [(outw, wout), (proj, wproj), (sel_l, vsel_l), (sel_e, vsel_e)]
    loads += [(sel_r, vsel_r), (sel_b, vsel_b), (target, vtarget), (mask, vmask)]
    copies = [pltpu.make_async_copy(a, b, local_sem.at[i]) for i, (a, b) in enumerate(loads)]
    for copy in copies:
        copy.start()

    copies[0].wait()
    copies[1].wait()
    lane = lax.broadcasted_iota(jnp.int32, (64, 128), 1)
    row64 = lax.broadcasted_iota(jnp.int32, (64, 128), 0)
    twice = jnp.where(lane % 64 == row64, 1.0, 0.0).astype(BF16)
    low = lane < 64
    taps = dot(wfilt[...], twice)

    def tap_of(layer, p, q):
        start = ((layer * 3 + p) * 3 + q) * 64
        return taps[start : start + 64]

    none = jnp.zeros((64, 128), F32)
    for jin in range(4):
        for jout in range(2):
            for kout in range(2):
                q = jin - jout
                base = (jout * 2 + kout) * 64
                rows = pl.ds(base, 64)
                if q < 0 or q > 2:
                    halves = (none, none)
                elif kout == 0:
                    halves = (jnp.where(low, tap_of(0, 0, q), tap_of(0, 1, q)), jnp.where(low, tap_of(0, 2, q), none))
                else:
                    halves = (jnp.where(low, none, tap_of(0, 0, q)), jnp.where(low, tap_of(0, 1, q), tap_of(0, 2, q)))
                first[rows, jin * 256 : jin * 256 + 128] = halves[0].astype(BF16)
                first[rows, jin * 256 + 128 : jin * 256 + 256] = halves[1].astype(BF16)

    head_row = vhead[0:1, :]
    h0 = head_row.astype(BF16).astype(F32)
    h1 = (head_row - h0).astype(BF16).astype(F32)
    h2 = (head_row - h0 - h1).astype(BF16).astype(F32)
    row8 = lax.broadcasted_iota(jnp.int32, (8, 64), 0)
    head8 = jnp.where(row8 == 0, h0, jnp.where(row8 == 1, h1, jnp.where(row8 == 2, h2, 0.0))).astype(BF16)
    head_twice = jnp.sum(dot(head8, twice), axis=0, keepdims=True)
    row96 = lax.broadcasted_iota(jnp.int32, (96, 128), 0)
    lane96 = lax.broadcasted_iota(jnp.int32, (96, 128), 1)
    k_out = row96 % 16
    kp = lane96 // 64
    q_of = row96 // 32

    def hi_lo(value):
        hi = value.astype(BF16).astype(F32)
        return hi, (value - hi).astype(BF16).astype(F32)

    folded = []
    for p in range(3):
        pieces = []
        for q in range(3):
            whole = jnp.sum(dot(head8, tap_of(1, p, q).astype(BF16)), axis=0, keepdims=True)
            for part in hi_lo(whole):
                pieces.append(jnp.broadcast_to(part, (16, 128)))
        folded.append(jnp.concatenate(pieces, axis=0))
    for m in range(9):
        p_of = 2 * m + kp - k_out
        block = jnp.zeros((96, 128), F32)
        for p in range(3):
            block = jnp.where(p_of == p, folded[p], block)
        gin[:, m * 128 : (m + 1) * 128] = block.astype(BF16)
    head_hi, head_lo = hi_lo(head_twice)
    head_block = jnp.where(row96 % 32 < 16, head_hi, head_lo)
    for m in range(8):
        block = jnp.where(jnp.logical_and(q_of == 1, 2 * m + kp == k_out), head_block, 0.0)
        gpair[:, m * 128 : (m + 1) * 128] = block.astype(BF16)

    for copy in copies[2:10]:
        copy.wait()
    for one in feat_moves:
        pl.when(on_diag(d + one[1]))(lambda one=one: feat_move(*one).wait_recv())

    def trunk(window, rows, start):
        at = lax.broadcasted_iota(jnp.int32, (rows, 1), 0) + start
        inside = jnp.logical_and(at >= 0, at < BINS)
        x = jnp.where(inside, window[...].astype(F32), 0.0)
        for layer, spread in ((0, 4), (1, 8)):
            y = dot(jnp.maximum(x, 0.0).astype(BF16), wconv[layer])
            c = pltpu.roll(y[:, 0:128], spread, 0) + y[:, 128:256] + pltpu.roll(y[:, 256:384], rows - spread, 0)
            v = jnp.maximum(c, 0.0).astype(BF16)
            x = jnp.where(inside, (x + dot(v, wout[layer])).astype(BF16).astype(F32), 0.0)
        value = dot(x.astype(BF16), wproj[...]).astype(BF16).astype(F32)
        return value, pltpu.roll(value, 64, 1)

    projected, swapped = trunk(win, ROWS, 128 * d - 32)

    for copy in copies[10:]:
        copy.wait()
    lane_l = lax.broadcasted_iota(jnp.int32, (ROWS, 128), 1) < 64
    left = jnp.where(lane_l, projected, swapped).astype(BF16)
    step_l = lax.broadcasted_iota(jnp.int32, (2, 288, 128), 1) // 16
    out_l = jnp.logical_or(jnp.logical_and(d == 0, step_l == 0), jnp.logical_and(d == N_DIAG - 1, step_l == 17))
    ll[...] = jnp.where(out_l, -1e30, dot(vsel_l[...], left).reshape(2, 288, 128))
    for one in embed_moves:
        pl.when(on_off(g + one[1]))(lambda one=one: embed_move(*one).wait_recv())
    erow = lax.broadcasted_iota(jnp.int32, (96, 64), 0) + 64 * g - 16
    e_in = jnp.logical_and(erow >= 0, erow < BAND)
    e_val = jnp.where(e_in, ewin[...].astype(F32), 0.0).astype(BF16)
    e_two = dot(e_val, twice)
    e_two = jnp.where(lane96 < 64, e_two, pltpu.roll(e_two, 92, 0)).astype(BF16)
    step_e = lax.broadcasted_iota(jnp.int32, (10, 16, 128), 0)
    out_e = jnp.logical_or(jnp.logical_and(g == 0, step_e == 0), jnp.logical_and(g == N_OFF - 1, step_e == 9))
    ee[...] = jnp.where(out_e, -1e30, dot(vsel_e[...], e_two).reshape(10, 16, 128))

    def right_finish(number, ahead, start, count, to):
        pl.when(jnp.logical_and(on_diag(d + ahead), ahead != 0))(
            lambda: right_move(number, ahead, start, count, to).wait_recv()
        )

    each_right(right_finish)

    def right_own(number, ahead, start, count, to):
        @pl.when(ahead == 0)
        def _():
            rwin[to : to + count, :] = win[32 + start : 32 + start + count, :]

    each_right(right_own)
    projected, swapped = trunk(rwin, W_RIGHT, 128 * d + 64 * g - 32)
    lane_r = lax.broadcasted_iota(jnp.int32, (W_RIGHT, 128), 1) < 64
    right = jnp.where(lane_r, swapped, pltpu.roll(projected, W_RIGHT - 4, 0)).astype(BF16)
    rr[...] = dot(vsel_r[...], right).reshape(2, 432, 128)

    for m in range(10):
        e = jnp.broadcast_to(ee[m][None], (18, 16, 128)).reshape(288, 128)
        for par in range(2):
            value = rr[par, m * 16 : m * 16 + 288, :] + ll[par] + e
            pair[par, :, m * 128 : (m + 1) * 128] = jnp.maximum(value, 0.0).astype(BF16)

    lane_n = lax.broadcasted_iota(jnp.int32, (272, 256), 1) % 128
    for m in range(9):
        cols = slice(m * 128, m * 128 + 256)
        near = jnp.concatenate(
            [pair[0, 0:272, cols], pair[1, 0:272, cols], pair[0, 16:288, cols], pair[1, 16:288, cols]], axis=1
        )
        acc = jnp.maximum(dot_nt(near, first[...]), 0.0)
        if m == 0:
            acc = jnp.where(jnp.logical_and(lane_n < 64, g == 0), 0.0, acc)
        if m == 8:
            acc = jnp.where(jnp.logical_and(lane_n >= 64, g == N_OFF - 1), 0.0, acc)
        acc = acc.astype(BF16)
        cols = slice(m * 128, (m + 1) * 128)
        inner[0, 0:16, cols] = jnp.where(d == 0, 0.0, acc[0:16, 0:128].astype(F32)).astype(BF16)
        inner[0, 16:272, cols] = acc[16:272, 0:128]
        inner[1, 0:256, cols] = acc[0:256, 128:256]
        inner[1, 256:272, cols] = jnp.where(d == N_DIAG - 1, 0.0, acc[256:272, 128:256].astype(F32)).astype(BF16)

    def turned(value):
        full = jnp.concatenate([value, jnp.zeros((256, 32), F32)], axis=1)
        return jnp.transpose(full)

    sums = []
    for par in range(2):
        t = dot_nt(inner[par], gin[...])
        t = t + dot_nt(pair[1 - par, 16 * par : 16 * par + 272, 128:1152], gpair[...])
        sums.append((turned(t[0:256]), turned(t[16:272])))

    def both(value, q):
        return value[32 * q : 32 * q + 16] + value[32 * q + 16 : 32 * q + 32]

    (a0, a1), (b0, b1) = sums
    even = both(a0, 0) + both(b0, 1) + both(a1, 2)
    odds = both(b0, 0) + both(a1, 1) + both(b1, 2)
    flat = jnp.concatenate([even, odds], axis=1)
    p0 = flat.astype(BF16).astype(F32)
    p1 = (flat - p0).astype(BF16).astype(F32)
    p2 = flat - p0 - p1
    stacked = jnp.concatenate([p0, p1, p2], axis=0).astype(BF16)
    placed = dot(stacked, vsel_b[...])
    placed = placed[0:16] + placed[16:32] + placed[32:48]
    for r in range(4):
        vpred[pl.ds(r, 16, stride=4), :] = placed[:, r * 128 : (r + 1) * 128]
    out_copy = pltpu.make_async_copy(vpred, pred, pred_sem)
    out_copy.start()

    o_of = lax.broadcasted_iota(jnp.int32, (64, 128), 0) + 64 * g
    i_of = lax.broadcasted_iota(jnp.int32, (64, 128), 1) + 128 * d
    valid = jnp.where(o_of + i_of < BINS, vmask[...].astype(F32), 0.0)
    err = valid * (vpred[...] - vtarget[...]) ** 2

    def spread(source, buf, steps, slot, peer, send, recv):
        for step in steps:
            pltpu.make_async_remote_copy(
                src_ref=source, dst_ref=buf.at[slot], send_sem=send, recv_sem=recv,
                device_id=peer(step), device_id_type=pl.DeviceIdType.MESH,
            ).start()

    def settled(buf, sem):
        pltpu.make_async_copy(buf.at[pl.ds(0, 15)], buf.at[pl.ds(0, 15)], sem).wait()

    red1[z_slot] = jnp.sum(err, axis=0, keepdims=True)
    spread(red1.at[z_slot], red1, z_steps, z_slot, z_peer, s1, r1)
    settled(red1, r1)
    vloss[...] = jnp.sum(red1[...], axis=0)
    spread(vloss, loss, xy_steps, xy_slot, xy_peer, s2, r2)
    own_part = pltpu.make_async_copy(vloss, loss.at[xy_slot], loss_sem)
    own_part.start()

    out_copy.wait()
    for one in feat_moves:
        pl.when(on_diag(d - one[1]))(lambda one=one: feat_move(*one).wait_send())
    for one in embed_moves:
        pl.when(on_off(g - one[1]))(lambda one=one: embed_move(*one).wait_send())

    def right_retire(number, ahead, start, count, to):
        pl.when(jnp.logical_and(on_diag(d - ahead), ahead != 0))(
            lambda: right_move(number, ahead, start, count, to).wait_send()
        )

    each_right(right_retire)
    settled(red1, s1)
    settled(loss, s2)
    own_part.wait()
    settled(loss, r2)


def finish(pred_in, parts, pred, loss):
    pred[...] = pred_in[...]
    loss[0, 0] = jnp.sum(parts[...]) / (BAND * BINS)


def body(features, conv_weight, out_weight, proj_weight, offset_embed, pair_filter_weight, head_weight, target, cell_mask):
    vmem = pl.BlockSpec(memory_space=pltpu.VMEM)
    anywhere = pl.BlockSpec(memory_space=pltpu.HBM)
    picks = [jnp.asarray(value) for value in selections()]
    pred, loss = pl.pallas_call(
        kernel,
        out_shape=(jax.ShapeDtypeStruct((64, 128), F32), jax.ShapeDtypeStruct((16, 1, 128), F32)),
        in_specs=[anywhere] * 13,
        out_specs=(anywhere, anywhere),
        scratch_shapes=[
            pltpu.VMEM((1, CP), F32),
            pltpu.VMEM((ROWS, D), BF16),
            pltpu.VMEM((96, CP), BF16),
            pltpu.VMEM((2, D, 384), BF16),
            pltpu.VMEM((2, 128, D), BF16),
            pltpu.VMEM((D, 128), BF16),
            pltpu.VMEM((1152, CP), BF16),
            pltpu.VMEM((64, 128), F32),
            pltpu.VMEM((64, 128), jnp.int32),
            pltpu.VMEM((864, W_RIGHT), BF16),
            pltpu.VMEM((576, ROWS), BF16),
            pltpu.VMEM((160, 96), BF16),
            pltpu.VMEM((512, 512), BF16),
            pltpu.VMEM((64, 128), F32),
            pltpu.VMEM((W_RIGHT, D), BF16),
            pltpu.VMEM((256, 1024), BF16),
            pltpu.VMEM((96, 1152), BF16),
            pltpu.VMEM((96, 1024), BF16),
            pltpu.VMEM((2, 432, 128), F32),
            pltpu.VMEM((2, 288, 128), F32),
            pltpu.VMEM((10, 16, 128), F32),
            pltpu.VMEM((2, 288, 1280), BF16),
            pltpu.VMEM((2, 272, 1152), BF16),
            pltpu.VMEM((16, 1, 128), F32),
            pltpu.SemaphoreType.DMA((18,)),
            pltpu.SemaphoreType.DMA((7,)),
            pltpu.SemaphoreType.DMA((7,)),
            pltpu.SemaphoreType.DMA,
            pltpu.SemaphoreType.DMA,
            pltpu.SemaphoreType.DMA,
            pltpu.SemaphoreType.DMA,
            pltpu.SemaphoreType.DMA,
            pltpu.VMEM((1, 128), F32),
            pltpu.SemaphoreType.DMA,
        ],
        compiler_params=pltpu.CompilerParams(
            collective_id=0, has_side_effects=True, vmem_limit_bytes=64 * 1024 * 1024
        ),
        name="contact_block",
    )(
        features, conv_weight, out_weight, proj_weight, offset_embed,
        pair_filter_weight.reshape(1152, CP), head_weight.reshape(1, CP), target, cell_mask, *picks,
    )
    pred, loss = pl.pallas_call(
        finish,
        out_shape=(jax.ShapeDtypeStruct((64, 128), F32), jax.ShapeDtypeStruct((1, 1), F32)),
        in_specs=[vmem, vmem],
        out_specs=(vmem, pl.BlockSpec(memory_space=pltpu.SMEM)),
        compiler_params=pltpu.CompilerParams(vmem_limit_bytes=64 * 1024 * 1024),
        name="finish",
    )(pred, loss)
    return pred, loss[0, 0]


def solution(mesh):
    in_specs = (P("diag", None), P(), P(), P(), P("off", None), P(), P(), P("off", "diag"), P("off", "diag"))
    out_specs = (P("off", "diag"), P())
    return jax.shard_map(body, mesh=mesh, in_specs=in_specs, out_specs=out_specs, check_vma=False)
```

```python
import jax
import jax.numpy as jnp
import ml_dtypes
import numpy as np
from jax import lax
from jax.experimental import pallas as pl
from jax.experimental.pallas import tpu as pltpu
from jax.sharding import PartitionSpec as P

BINS = 4096
BAND = 512
CP = 64
D = 256
N_DIAG = 32
N_OFF = 8
ROWS = 192
W_RIGHT = 256
F32 = jnp.float32
BF16 = jnp.bfloat16
NT = (((1,), (1,)), ((), ()))


def selections():
    def one_hot(index, width):
        index = np.asarray(index).reshape(-1)
        return (index[:, None] == np.arange(width)[None, :]).astype(ml_dtypes.bfloat16)

    par, v, r, s = np.meshgrid(np.arange(2), np.arange(27), np.arange(4), np.arange(4), indexing="ij")
    right = one_hot(4 * (2 * v + par) + r + s + 16, W_RIGHT)
    par, jj, r, s = np.meshgrid(np.arange(2), np.arange(18), np.arange(4), np.arange(4), indexing="ij")
    left = one_hot(4 * (2 * jj + par) + s + 24, ROWS)
    m, r, s = np.meshgrid(np.arange(10), np.arange(4), np.arange(4), indexing="ij")
    embed = one_hot(8 * m + r + 8, 96)
    jo, jj, r, s = np.meshgrid(np.arange(2), np.arange(16), np.arange(4), np.arange(4), indexing="ij")
    back = one_hot(r * 128 + 4 * (2 * jj + jo) + s, 512)
    return right, left, embed, back


def dot(a, b):
    return jnp.dot(a, b, preferred_element_type=F32)


def dot_nt(a, b):
    return lax.dot_general(a, b, NT, preferred_element_type=F32)


def kernel(
    feat, conv, outw, proj, emb, filt, head, target, mask, sel_r, sel_l, sel_e, sel_b,
    pred, loss,
    vhead, win, ewin, wconv, wout, wproj, wfilt, vtarget, vmask, vsel_r, vsel_l, vsel_e, vsel_b, vpred,
    rwin, first, gin, gpair, rr, ll, ee, pair, inner, red1,
    local_sem, send_sem, recv_sem, pred_sem, s1, r1, s2, r2, vloss, loss_sem,
):
    d = lax.axis_index("diag")
    g = lax.axis_index("off")
    h = g // 2
    odd = g % 2
    core = odd
    z_lo = d // 16
    xy = d % 16
    x_at = xy // 4
    y_at = xy % 4
    z_at = 2 * h + z_lo

    feat_moves = [(0, -1, 96, 0), (1, 1, 0, 160)]
    embed_moves = [(2, -1, 48, 0), (3, 1, 0, 80)]
    even_moves = [(5, h, 0, 128, 32), (6, h + 1, 0, 96, 160), (4, h - 1, 96, 32, 0)]
    odd_moves = [(5, h + 1, 0, 128, 96), (4, h, 32, 96, 0), (6, h + 2, 0, 32, 224)]

    def on_diag(index):
        return jnp.logical_and(index >= 0, index < N_DIAG)

    def on_off(index):
        return jnp.logical_and(index >= 0, index < N_OFF)

    def remote(src, dst, number, peer):
        return pltpu.make_async_remote_copy(
            src_ref=src, dst_ref=dst, send_sem=send_sem.at[number], recv_sem=recv_sem.at[number],
            device_id=peer, device_id_type=pl.DeviceIdType.MESH,
        )

    def feat_move(number, ahead, start, to):
        return remote(win.at[pl.ds(32 + start, 32)], win.at[pl.ds(to, 32)], number, (d - ahead, g))

    def embed_move(number, ahead, start, to):
        return remote(ewin.at[pl.ds(16 + start, 16)], ewin.at[pl.ds(to, 16)], number, (d, g - ahead))

    def right_move(number, ahead, start, count, to):
        return remote(win.at[pl.ds(32 + start, count)], rwin.at[pl.ds(to, count)], number, (d - ahead, g))

    def each_right(act):
        pl.when(odd == 0)(lambda: [act(*one) for one in even_moves] and None)
        pl.when(odd == 1)(lambda: [act(*one) for one in odd_moves] and None)

    def wrapped(value, size):
        return jnp.where(value >= size, value - size, value)

    def far(step, size):
        return min(step, size - step)

    z_steps = sorted(((a, b) for a in range(8) for b in range(2) if a or b), key=lambda t: -far(t[0], 8) * 2 - t[1])
    xy_steps = sorted(((a, b) for a in range(4) for b in range(4) if a or b), key=lambda t: -far(t[0], 4) - far(t[1], 4))

    def z_peer(step):
        z = wrapped(z_at + step[0], 8)
        c = wrapped(core + step[1], 2)
        return (z % 2 * 16 + xy, z // 2 * 2 + c)

    def xy_peer(step):
        return (z_lo * 16 + wrapped(x_at + step[0], 4) * 4 + wrapped(y_at + step[1], 4), g)

    z_slot = z_at * 2 + core
    xy_slot = xy

    own = [
        pltpu.make_async_copy(feat, win.at[pl.ds(32, 128)], local_sem.at[16]),
        pltpu.make_async_copy(emb, ewin.at[pl.ds(16, 64)], local_sem.at[17]),
    ]
    for copy in own:
        copy.start()
    barrier = pltpu.get_barrier_semaphore()

    def greet(peer, times=1):
        pl.semaphore_signal(barrier, inc=times, device_id=peer, device_id_type=pl.DeviceIdType.MESH)

    def count_of(cond):
        return jnp.where(cond, 1, 0).astype(jnp.int32)

    for step in z_steps:
        greet(z_peer(step))
    total = jnp.int32(30)
    for reach in (-1, 1):
        ok = on_diag(d - reach)
        pl.when(ok)(lambda reach=reach: greet((d - reach, g)))
        total = total + count_of(ok)
        ok = on_off(g - reach)
        pl.when(ok)(lambda reach=reach: greet((d, g - reach)))
        total = total + count_of(ok)
    for step in range(3):
        ahead = h - 1 + odd + step
        ok_s = jnp.logical_and(on_diag(d - ahead), ahead != 0)
        ok_r = jnp.logical_and(on_diag(d + ahead), ahead != 0)
        pl.when(ok_s)(lambda ahead=ahead: greet((d - ahead, g)))
        pl.when(ok_r)(lambda ahead=ahead: greet((d + ahead, g)))
        total = total + count_of(ok_s) + count_of(ok_r)
    for step in xy_steps:
        greet(xy_peer(step))

    def right_begin(number, ahead, start, count, to):
        pl.when(jnp.logical_and(on_diag(d - ahead), ahead != 0))(
            lambda: right_move(number, ahead, start, count, to).start()
        )

    for copy in own:
        copy.wait()
    pl.semaphore_wait(barrier, total)
    for one in feat_moves:
        pl.when(on_diag(d - one[1]))(lambda one=one: feat_move(*one).start())
    each_right(right_begin)
    for one in embed_moves:
        pl.when(on_off(g - one[1]))(lambda one=one: embed_move(*one).start())

    loads = [(filt, wfilt), (head, vhead)]
    for layer in range(2):
        for tap in range(3):
            loads.append((conv.at[layer, tap], wconv.at[layer, :, pl.ds(128 * tap, 128)]))
    loads += [(outw, wout), (proj, wproj), (sel_l, vsel_l), (sel_e, vsel_e)]
    loads += [(sel_r, vsel_r), (sel_b, vsel_b), (target, vtarget), (mask, vmask)]
    copies = [pltpu.make_async_copy(a, b, local_sem.at[i]) for i, (a, b) in enumerate(loads)]
    for copy in copies:
        copy.start()

    copies[0].wait()
    copies[1].wait()
    lane = lax.broadcasted_iota(jnp.int32, (64, 128), 1)
    row64 = lax.broadcasted_iota(jnp.int32, (64, 128), 0)
    twice = jnp.where(lane % 64 == row64, 1.0, 0.0).astype(BF16)
    low = lane < 64
    taps = dot(wfilt[...], twice)

    def tap_of(layer, p, q):
        start = ((layer * 3 + p) * 3 + q) * 64
        return taps[start : start + 64]

    none = jnp.zeros((64, 128), F32)
    for jin in range(4):
        for jout in range(2):
            for kout in range(2):
                q = jin - jout
                base = (jout * 2 + kout) * 64
                rows = pl.ds(base, 64)
                if q < 0 or q > 2:
                    halves = (none, none)
                elif kout == 0:
                    halves = (jnp.where(low, tap_of(0, 0, q), tap_of(0, 1, q)), jnp.where(low, tap_of(0, 2, q), none))
                else:
                    halves = (jnp.where(low, none, tap_of(0, 0, q)), jnp.where(low, tap_of(0, 1, q), tap_of(0, 2, q)))
                first[rows, jin * 256 : jin * 256 + 128] = halves[0].astype(BF16)
                first[rows, jin * 256 + 128 : jin * 256 + 256] = halves[1].astype(BF16)

    head_row = vhead[0:1, :]
    h0 = head_row.astype(BF16).astype(F32)
    h1 = (head_row - h0).astype(BF16).astype(F32)
    h2 = (head_row - h0 - h1).astype(BF16).astype(F32)
    row8 = lax.broadcasted_iota(jnp.int32, (8, 64), 0)
    head8 = jnp.where(row8 == 0, h0, jnp.where(row8 == 1, h1, jnp.where(row8 == 2, h2, 0.0))).astype(BF16)
    head_twice = jnp.sum(dot(head8, twice), axis=0, keepdims=True)
    row96 = lax.broadcasted_iota(jnp.int32, (96, 128), 0)
    lane96 = lax.broadcasted_iota(jnp.int32, (96, 128), 1)
    k_out = row96 % 16
    kp = lane96 // 64
    q_of = row96 // 32

    def hi_lo(value):
        hi = value.astype(BF16).astype(F32)
        return hi, (value - hi).astype(BF16).astype(F32)

    folded = []
    for p in range(3):
        pieces = []
        for q in range(3):
            whole = jnp.sum(dot(head8, tap_of(1, p, q).astype(BF16)), axis=0, keepdims=True)
            for part in hi_lo(whole):
                pieces.append(jnp.broadcast_to(part, (16, 128)))
        folded.append(jnp.concatenate(pieces, axis=0))
    for m in range(9):
        p_of = 2 * m + kp - k_out
        block = jnp.zeros((96, 128), F32)
        for p in range(3):
            block = jnp.where(p_of == p, folded[p], block)
        gin[:, m * 128 : (m + 1) * 128] = block.astype(BF16)
    head_hi, head_lo = hi_lo(head_twice)
    head_block = jnp.where(row96 % 32 < 16, head_hi, head_lo)
    for m in range(8):
        block = jnp.where(jnp.logical_and(q_of == 1, 2 * m + kp == k_out), head_block, 0.0)
        gpair[:, m * 128 : (m + 1) * 128] = block.astype(BF16)

    for copy in copies[2:10]:
        copy.wait()
    for one in feat_moves:
        pl.when(on_diag(d + one[1]))(lambda one=one: feat_move(*one).wait_recv())

    def trunk(window, rows, start):
        at = lax.broadcasted_iota(jnp.int32, (rows, 1), 0) + start
        inside = jnp.logical_and(at >= 0, at < BINS)
        x = jnp.where(inside, window[...].astype(F32), 0.0)
        for layer, spread in ((0, 4), (1, 8)):
            y = dot(jnp.maximum(x, 0.0).astype(BF16), wconv[layer])
            c = pltpu.roll(y[:, 0:128], spread, 0) + y[:, 128:256] + pltpu.roll(y[:, 256:384], rows - spread, 0)
            v = jnp.maximum(c, 0.0).astype(BF16)
            x = jnp.where(inside, (x + dot(v, wout[layer])).astype(BF16).astype(F32), 0.0)
        value = dot(x.astype(BF16), wproj[...]).astype(BF16).astype(F32)
        return value, pltpu.roll(value, 64, 1)

    projected, swapped = trunk(win, ROWS, 128 * d - 32)

    def right_own(number, ahead, start, count, to):
        @pl.when(ahead == 0)
        def _():
            rwin[to : to + count, :] = win[32 + start : 32 + start + count, :]

    each_right(right_own)

    for copy in copies[10:]:
        copy.wait()
    lane_l = lax.broadcasted_iota(jnp.int32, (ROWS, 128), 1) < 64
    left = jnp.where(lane_l, projected, swapped).astype(BF16)
    step_l = lax.broadcasted_iota(jnp.int32, (2, 288, 128), 1) // 16
    out_l = jnp.logical_or(jnp.logical_and(d == 0, step_l == 0), jnp.logical_and(d == N_DIAG - 1, step_l == 17))
    ll[...] = jnp.where(out_l, -1e30, dot(vsel_l[...], left).reshape(2, 288, 128))
    for one in embed_moves:
        pl.when(on_off(g + one[1]))(lambda one=one: embed_move(*one).wait_recv())
    erow = lax.broadcasted_iota(jnp.int32, (96, 64), 0) + 64 * g - 16
    e_in = jnp.logical_and(erow >= 0, erow < BAND)
    e_val = jnp.where(e_in, ewin[...].astype(F32), 0.0).astype(BF16)
    e_two = dot(e_val, twice)
    e_two = jnp.where(lane96 < 64, e_two, pltpu.roll(e_two, 92, 0)).astype(BF16)
    step_e = lax.broadcasted_iota(jnp.int32, (10, 16, 128), 0)
    out_e = jnp.logical_or(jnp.logical_and(g == 0, step_e == 0), jnp.logical_and(g == N_OFF - 1, step_e == 9))
    ee[...] = jnp.where(out_e, -1e30, dot(vsel_e[...], e_two).reshape(10, 16, 128))

    def right_finish(number, ahead, start, count, to):
        pl.when(jnp.logical_and(on_diag(d + ahead), ahead != 0))(
            lambda: right_move(number, ahead, start, count, to).wait_recv()
        )

    each_right(right_finish)

    projected, swapped = trunk(rwin, W_RIGHT, 128 * d + 64 * g - 32)
    lane_r = lax.broadcasted_iota(jnp.int32, (W_RIGHT, 128), 1) < 64
    right = jnp.where(lane_r, swapped, pltpu.roll(projected, W_RIGHT - 4, 0)).astype(BF16)
    rr[...] = dot(vsel_r[...], right).reshape(2, 432, 128)

    for m in range(10):
        e = jnp.broadcast_to(ee[m][None], (18, 16, 128)).reshape(288, 128)
        for par in range(2):
            value = rr[par, m * 16 : m * 16 + 288, :] + ll[par] + e
            pair[par, :, m * 128 : (m + 1) * 128] = jnp.maximum(value, 0.0).astype(BF16)

    lane_n = lax.broadcasted_iota(jnp.int32, (272, 256), 1) % 128
    for m in range(9):
        cols = slice(m * 128, m * 128 + 256)
        near = jnp.concatenate(
            [pair[0, 0:272, cols], pair[1, 0:272, cols], pair[0, 16:288, cols], pair[1, 16:288, cols]], axis=1
        )
        acc = jnp.maximum(dot_nt(near, first[...]), 0.0)
        if m == 0:
            acc = jnp.where(jnp.logical_and(lane_n < 64, g == 0), 0.0, acc)
        if m == 8:
            acc = jnp.where(jnp.logical_and(lane_n >= 64, g == N_OFF - 1), 0.0, acc)
        acc = acc.astype(BF16)
        cols = slice(m * 128, (m + 1) * 128)
        inner[0, 0:16, cols] = jnp.where(d == 0, 0.0, acc[0:16, 0:128].astype(F32)).astype(BF16)
        inner[0, 16:272, cols] = acc[16:272, 0:128]
        inner[1, 0:256, cols] = acc[0:256, 128:256]
        inner[1, 256:272, cols] = jnp.where(d == N_DIAG - 1, 0.0, acc[256:272, 128:256].astype(F32)).astype(BF16)

    def turned(value):
        full = jnp.concatenate([value, jnp.zeros((256, 32), F32)], axis=1)
        return jnp.transpose(full)

    sums = []
    for par in range(2):
        t = dot_nt(inner[par], gin[...])
        t = t + dot_nt(pair[1 - par, 16 * par : 16 * par + 272, 128:1152], gpair[...])
        sums.append((turned(t[0:256]), turned(t[16:272])))

    def both(value, q):
        return value[32 * q : 32 * q + 16] + value[32 * q + 16 : 32 * q + 32]

    (a0, a1), (b0, b1) = sums
    even = both(a0, 0) + both(b0, 1) + both(a1, 2)
    odds = both(b0, 0) + both(a1, 1) + both(b1, 2)
    flat = jnp.concatenate([even, odds], axis=1)
    p0 = flat.astype(BF16).astype(F32)
    p1 = (flat - p0).astype(BF16).astype(F32)
    p2 = flat - p0 - p1
    stacked = jnp.concatenate([p0, p1, p2], axis=0).astype(BF16)
    placed = dot(stacked, vsel_b[...])
    placed = placed[0:16] + placed[16:32] + placed[32:48]
    for r in range(4):
        vpred[pl.ds(r, 16, stride=4), :] = placed[:, r * 128 : (r + 1) * 128]
    out_copy = pltpu.make_async_copy(vpred, pred, pred_sem)
    out_copy.start()

    o_of = lax.broadcasted_iota(jnp.int32, (64, 128), 0) + 64 * g
    i_of = lax.broadcasted_iota(jnp.int32, (64, 128), 1) + 128 * d
    valid = jnp.where(o_of + i_of < BINS, vmask[...].astype(F32), 0.0)
    err = valid * (vpred[...] - vtarget[...]) ** 2

    def spread(source, buf, steps, slot, peer, send, recv):
        for step in steps:
            pltpu.make_async_remote_copy(
                src_ref=source, dst_ref=buf.at[slot], send_sem=send, recv_sem=recv,
                device_id=peer(step), device_id_type=pl.DeviceIdType.MESH,
            ).start()

    def settled(buf, sem):
        pltpu.make_async_copy(buf.at[pl.ds(0, 15)], buf.at[pl.ds(0, 15)], sem).wait()

    red1[z_slot] = jnp.sum(err, axis=0, keepdims=True)
    spread(red1.at[z_slot], red1, z_steps, z_slot, z_peer, s1, r1)
    settled(red1, r1)
    vloss[...] = jnp.sum(red1[...], axis=0)
    spread(vloss, loss, xy_steps, xy_slot, xy_peer, s2, r2)
    own_part = pltpu.make_async_copy(vloss, loss.at[xy_slot], loss_sem)
    own_part.start()

    out_copy.wait()
    for one in feat_moves:
        pl.when(on_diag(d - one[1]))(lambda one=one: feat_move(*one).wait_send())
    for one in embed_moves:
        pl.when(on_off(g - one[1]))(lambda one=one: embed_move(*one).wait_send())

    def right_retire(number, ahead, start, count, to):
        pl.when(jnp.logical_and(on_diag(d - ahead), ahead != 0))(
            lambda: right_move(number, ahead, start, count, to).wait_send()
        )

    each_right(right_retire)
    settled(red1, s1)
    settled(loss, s2)
    own_part.wait()
    settled(loss, r2)


def finish(pred_in, parts, pred, loss):
    pred[...] = pred_in[...]
    loss[0, 0] = jnp.sum(parts[...]) / (BAND * BINS)


def body(features, conv_weight, out_weight, proj_weight, offset_embed, pair_filter_weight, head_weight, target, cell_mask):
    vmem = pl.BlockSpec(memory_space=pltpu.VMEM)
    anywhere = pl.BlockSpec(memory_space=pltpu.HBM)
    picks = [jnp.asarray(value) for value in selections()]
    pred, loss = pl.pallas_call(
        kernel,
        out_shape=(jax.ShapeDtypeStruct((64, 128), F32), jax.ShapeDtypeStruct((16, 1, 128), F32)),
        in_specs=[anywhere] * 13,
        out_specs=(anywhere, anywhere),
        scratch_shapes=[
            pltpu.VMEM((1, CP), F32),
            pltpu.VMEM((ROWS, D), BF16),
            pltpu.VMEM((96, CP), BF16),
            pltpu.VMEM((2, D, 384), BF16),
            pltpu.VMEM((2, 128, D), BF16),
            pltpu.VMEM((D, 128), BF16),
            pltpu.VMEM((1152, CP), BF16),
            pltpu.VMEM((64, 128), F32),
            pltpu.VMEM((64, 128), jnp.int32),
            pltpu.VMEM((864, W_RIGHT), BF16),
            pltpu.VMEM((576, ROWS), BF16),
            pltpu.VMEM((160, 96), BF16),
            pltpu.VMEM((512, 512), BF16),
            pltpu.VMEM((64, 128), F32),
            pltpu.VMEM((W_RIGHT, D), BF16),
            pltpu.VMEM((256, 1024), BF16),
            pltpu.VMEM((96, 1152), BF16),
            pltpu.VMEM((96, 1024), BF16),
            pltpu.VMEM((2, 432, 128), F32),
            pltpu.VMEM((2, 288, 128), F32),
            pltpu.VMEM((10, 16, 128), F32),
            pltpu.VMEM((2, 288, 1280), BF16),
            pltpu.VMEM((2, 272, 1152), BF16),
            pltpu.VMEM((16, 1, 128), F32),
            pltpu.SemaphoreType.DMA((18,)),
            pltpu.SemaphoreType.DMA((7,)),
            pltpu.SemaphoreType.DMA((7,)),
            pltpu.SemaphoreType.DMA,
            pltpu.SemaphoreType.DMA,
            pltpu.SemaphoreType.DMA,
            pltpu.SemaphoreType.DMA,
            pltpu.SemaphoreType.DMA,
            pltpu.VMEM((1, 128), F32),
            pltpu.SemaphoreType.DMA,
        ],
        compiler_params=pltpu.CompilerParams(
            collective_id=0, has_side_effects=True, vmem_limit_bytes=64 * 1024 * 1024
        ),
        name="contact_block",
    )(
        features, conv_weight, out_weight, proj_weight, offset_embed,
        pair_filter_weight.reshape(1152, CP), head_weight.reshape(1, CP), target, cell_mask, *picks,
    )
    pred, loss = pl.pallas_call(
        finish,
        out_shape=(jax.ShapeDtypeStruct((64, 128), F32), jax.ShapeDtypeStruct((1, 1), F32)),
        in_specs=[vmem, vmem],
        out_specs=(vmem, pl.BlockSpec(memory_space=pltpu.SMEM)),
        compiler_params=pltpu.CompilerParams(vmem_limit_bytes=64 * 1024 * 1024),
        name="finish",
    )(pred, loss)
    return pred, loss[0, 0]


def solution(mesh):
    in_specs = (P("diag", None), P(), P(), P(), P("off", None), P(), P(), P("off", "diag"), P("off", "diag"))
    out_specs = (P("off", "diag"), P())
    return jax.shard_map(body, mesh=mesh, in_specs=in_specs, out_specs=out_specs, check_vma=False)
```
